32 devices in a mesh: groups: 2 (over x), crate: 16 (over z, y, core).
Axes of the slice: x: 2, y: 2, z: 4, core: 2. Of those that a mesh axis runs over, the one named last changes fastest.
Arguments:
- voltages: bfloat16 [4096, 17920], P(('groups', 'crate')), parts along dimension 0, may hold values from -6 to 6
- gains: float32 [256, 2, 2048], P('crate'), may hold values from -4 to 4
- positions: float32 [3, 2048], replicated, may hold values from -64 to 64
- directions: float32 [3, 512], replicated, may hold values from -0.5 to 0.5
- input_order: int32 [2048], replicated, may hold values from 0 to 2047, each once
- delays: int32 [1024, 256], replicated, may hold values from 0 to 31
- search_beams: int32 [16], replicated, may hold values from 0 to 511, as said below
Outputs:
- beam_power: float32 [512, 512, 32], P(('groups', 'crate')), parts along dimension 0
- dm_plane: float32 [2048, 16, 32], P(('groups', 'crate')), parts along dimension 0
The draws below stay inside these ranges and needn't reach their ends.
There are 2 independent parts, one for each index of `groups`. The reference program is written for one: setup_inputs(seed, part) draws one part's arguments, and reference() takes and returns one part's arrays. A program takes and returns all parts, laid end to end along the dimension named above; an argument that names none is the same for every part. Nothing has to cross between parts.
Inputs may be any that keep to these rules, and one draw needn't show every extreme that they name: `input_order`: each antenna is carried by exactly one input row. `search_beams`: 16 distinct beams, among them beam 0 and beam 512 - 1.
All inputs are finite; a program needn't handle non-finite values.
Results may differ from the reference program's by a relative error of at most 0.0082.
Values may be sent and summed in bfloat16 or wider, within the bound.
A program may use at most 64 MiB of HBM per device.

```python
import math
import jax
import jax.numpy as jnp
from jax import lax

INPUTS = 2048
CH = 256
BEAMS = 512
TRIALS = 1024
TAPS = 4
TIME = 32
SEARCH = 16
FFTLEN = 512
SAMPLES = 17920
N_CRATE = 16


def draw_search_beams(key, part):
    key_pick, key_order = jax.random.split(jax.random.fold_in(key, 17))
    interior = 1 + jax.random.permutation(key_pick, BEAMS - 2)[:SEARCH - 2]
    listed = jnp.concatenate([jnp.array([0, BEAMS - 1], dtype=jnp.int32), interior.astype(jnp.int32)])
    return listed[jax.random.permutation(key_order, SEARCH)]


def place_ends(values, rng, smallest, high):
    longest = values.shape.index(max(values.shape))
    spots = []
    for shift in (0, 1):
        where = [jax.random.randint(jax.random.fold_in(rng, axis), (), 0, length) for axis, length in enumerate(values.shape)]
        where[longest] = (where[longest] + shift) % values.shape[longest]
        spots.append(tuple(where))
    return values.at[spots[0]].set(smallest).at[spots[1]].set(high)


def levels(rng, shape, cuts, smallest, top_value):
    factor_of, own = 1.0, jax.random.fold_in(rng, 6)
    for dim, shards_of in cuts:
        steps = jnp.exp(jax.random.uniform(jax.random.fold_in(own, dim), (shards_of,), jnp.float32, smallest / len(cuts), top_value / len(cuts)))
        factor_of = factor_of * jnp.repeat(steps, shape[dim] // shards_of).reshape([-1 if axis == dim else 1 for axis in range(len(shape))])
    return factor_of


def bell_draw(stream_key, shape, scale, reach, cuts=(), held_as=jnp.bfloat16):
    entries = scale * jax.random.normal(stream_key, shape, jnp.float32)
    if cuts:
        entries = entries * levels(stream_key, shape, cuts, -0.22, 0.18)
    return jnp.clip(entries, -reach, reach).astype(held_as)


def setup_inputs(seed: int = 0, part: int = 0) -> dict:
    key_list = jax.random.split(jax.random.key(seed), 8)
    own_keys = jax.random.split(jax.random.fold_in(key_list[7], part), 8)
    voltages = bell_draw(own_keys[0], (INPUTS, SAMPLES), 1.0, 6.0, ((0, 16),))
    gains = bell_draw(key_list[1], (CH, 2, INPUTS), 0.7, 4.0, ((0, 16),), jnp.float32)
    positions = jnp.clip(jax.random.uniform(key_list[2], (3, INPUTS), jnp.float32, -64.0, 64.0), -64.0, 64.0)
    directions = jnp.clip(jax.random.uniform(key_list[3], (3, BEAMS), jnp.float32, -0.5, 0.5), -0.5, 0.5)
    input_order = jax.random.permutation(key_list[4], INPUTS).astype(jnp.int32)
    delays = place_ends(jax.random.randint(key_list[5], (TRIALS, CH), 0, TIME), jax.random.fold_in(key_list[5], 1), 0, TIME - 1).astype(jnp.int32)
    search_beams = draw_search_beams(jax.random.fold_in(key_list[7], 71), part)
    return {"voltages": voltages, "gains": gains, "positions": positions, "directions": directions, "input_order": input_order, "delays": delays, "search_beams": search_beams}


TWO_PI = 2.0 * math.pi

def pfb_window():
    window_len = TAPS * FFTLEN
    sample_index = jnp.arange(window_len, dtype=jnp.int32).astype(jnp.float32)
    offsets = (sample_index - 0.5 * window_len + 0.5) / FFTLEN
    tapering = 0.54 - 0.46 * jnp.cos(TWO_PI * sample_index / (window_len - 1))
    return (jnp.sinc(offsets) * tapering).reshape(TAPS, FFTLEN)

def fold_frames(voltages, window):
    frames = voltages.reshape(voltages.shape[0], TIME + TAPS - 1, FFTLEN)
    summed = window[0] * frames[:, 0:TIME].astype(jnp.float32)
    for tap_index in range(1, TAPS):
        summed = summed + window[tap_index] * frames[:, tap_index:tap_index + TIME].astype(jnp.float32)
    return summed.astype(jnp.bfloat16)

def dft_table():
    channel_ids = jnp.arange(CH, dtype=jnp.int32)[:, None]
    sample_ids = jnp.arange(FFTLEN, dtype=jnp.int32)[None, :]
    angles = TWO_PI * (channel_ids * sample_ids % FFTLEN).astype(jnp.float32) / FFTLEN
    factor = 1.0 / math.sqrt(FFTLEN)
    stacked = jnp.stack([jnp.cos(angles) * factor, -jnp.sin(angles) * factor], axis=1)
    return stacked.reshape(2 * CH, FFTLEN).astype(jnp.bfloat16)

def time_table():
    step_ids = jnp.arange(TIME, dtype=jnp.int32)[:, None]
    bin_ids = jnp.arange(1, TIME // 2 + 1, dtype=jnp.int32)[None, :]
    angles = TWO_PI * (step_ids * bin_ids % TIME).astype(jnp.float32) / TIME
    factor = 1.0 / math.sqrt(TIME)
    return jnp.concatenate([jnp.cos(angles) * factor, -jnp.sin(angles) * factor], axis=1)

def array_geometry(positions, directions, input_order):
    placed = jnp.take(positions, input_order, axis=1)
    geometry = directions[0][:, None] * placed[0][None, :]
    geometry = geometry + directions[1][:, None] * placed[1][None, :]
    return geometry + directions[2][:, None] * placed[2][None, :]

def steering(geometry, gain_row, frequency):
    phases = TWO_PI * frequency * geometry
    cosine = jnp.cos(phases)
    sine_part = jnp.sin(phases)
    weight_norm = 1.0 / math.sqrt(INPUTS)
    w_real = ((gain_row[0] * cosine + gain_row[1] * sine_part) * weight_norm).astype(jnp.bfloat16)
    w_imag = ((gain_row[1] * cosine - gain_row[0] * sine_part) * weight_norm).astype(jnp.bfloat16)
    upper_rows = jnp.concatenate([w_real, -w_imag], axis=1)
    lower_rows = jnp.concatenate([w_imag, w_real], axis=1)
    return jnp.concatenate([upper_rows, lower_rows], axis=0)

def dedisperse(spectrum, delay_part):
    half_bins = TIME // 2
    bin_ids = jnp.arange(1, half_bins + 1, dtype=jnp.int32)
    turn_counts = delay_part[:, :, None] * bin_ids[None, None, :] % TIME
    angles = TWO_PI * turn_counts.astype(jnp.float32) / TIME
    cosine = jnp.cos(angles)
    sine_part = jnp.sin(angles)
    spec_real = spectrum[:, :, :half_bins]
    spec_imag = spectrum[:, :, half_bins:]
    highest = lax.Precision.HIGHEST
    out_real = jnp.einsum('cbk,dck->dbk', spec_real, cosine, precision=highest) - jnp.einsum('cbk,dck->dbk', spec_imag, sine_part, precision=highest)
    out_imag = jnp.einsum('cbk,dck->dbk', spec_real, sine_part, precision=highest) + jnp.einsum('cbk,dck->dbk', spec_imag, cosine, precision=highest)
    factor = 1.0 / math.sqrt(CH)
    return jnp.concatenate([out_real, out_imag], axis=2) * factor

def reference(voltages, gains, positions, directions, input_order, delays, search_beams):
    window = pfb_window()
    dft_rows = dft_table().astype(jnp.float32)
    blocks = voltages.reshape(N_CRATE, INPUTS // N_CRATE, SAMPLES)

    def channelize(block_volts):
        folded = fold_frames(block_volts, window)
        spectra_block = jnp.einsum('ks,its->kit', dft_rows, folded.astype(jnp.float32))
        return spectra_block.astype(jnp.bfloat16)
    spectra = lax.map(channelize, blocks)
    spectra = jnp.moveaxis(spectra, 0, 1).reshape(CH, 2, INPUTS, TIME)
    geometry = array_geometry(positions, directions, input_order)

    def one_channel(packed):
        channel, channel_data, gain_row = packed
        frequency = 1.0 + channel.astype(jnp.float32) / CH
        weights = steering(geometry, gain_row, frequency)
        beam_sums = jnp.dot(weights, channel_data.reshape(2 * INPUTS, TIME), preferred_element_type=jnp.float32)
        return beam_sums[:BEAMS] * beam_sums[:BEAMS] + beam_sums[BEAMS:] * beam_sums[BEAMS:]
    beam_power = lax.map(one_channel, (jnp.arange(CH, dtype=jnp.int32), spectra, gains))
    chosen = jnp.take(beam_power, search_beams, axis=1)
    power_spectra = jnp.dot(chosen.reshape(CH * SEARCH, TIME), time_table(), precision=lax.Precision.HIGHEST, preferred_element_type=jnp.float32)
    power_spectra = power_spectra.reshape(CH, SEARCH, TIME)
    dm_plane = dedisperse(power_spectra, delays)
    return (beam_power, dm_plane)
```

```python
import functools
import math

import jax
import jax.numpy as jnp
import numpy as np
from jax import lax
from jax.experimental import pallas as pl
from jax.experimental.pallas import tpu as pltpu
from jax.sharding import PartitionSpec as P

INPUTS = 2048
CH = 256
BEAMS = 512
TRIALS = 1024
TAPS = 4
TIME = 32
SEARCH = 16
FFTLEN = 512


TWO_PI = 2.0 * math.pi


def pfb_window():
    window_len = TAPS * FFTLEN
    sample_index = jnp.arange(window_len, dtype=jnp.int32).astype(jnp.float32)
    offsets = (sample_index - 0.5 * window_len + 0.5) / FFTLEN
    tapering = 0.54 - 0.46 * jnp.cos(TWO_PI * sample_index / (window_len - 1))
    return (jnp.sinc(offsets) * tapering).reshape(TAPS, FFTLEN)


def fold_frames(voltages, window):
    frames = voltages.reshape(voltages.shape[0], TIME + TAPS - 1, FFTLEN)
    summed = window[0] * frames[:, 0:TIME].astype(jnp.float32)
    for tap_index in range(1, TAPS):
        summed = summed + window[tap_index] * frames[:, tap_index : tap_index + TIME].astype(
            jnp.float32
        )
    return summed.astype(jnp.bfloat16)


def dft_table():
    channel_ids = jnp.arange(CH, dtype=jnp.int32)[:, None]
    sample_ids = jnp.arange(FFTLEN, dtype=jnp.int32)[None, :]
    angles = TWO_PI * (channel_ids * sample_ids % FFTLEN).astype(jnp.float32) / FFTLEN
    factor = 1.0 / math.sqrt(FFTLEN)
    stacked = jnp.stack([jnp.cos(angles) * factor, -jnp.sin(angles) * factor], axis=1)
    return stacked.reshape(2 * CH, FFTLEN).astype(jnp.bfloat16)


def time_table():
    step_ids = jnp.arange(TIME, dtype=jnp.int32)[:, None]
    bin_ids = jnp.arange(1, TIME // 2 + 1, dtype=jnp.int32)[None, :]
    angles = TWO_PI * (step_ids * bin_ids % TIME).astype(jnp.float32) / TIME
    factor = 1.0 / math.sqrt(TIME)
    return jnp.concatenate([jnp.cos(angles) * factor, -jnp.sin(angles) * factor], axis=1)


def array_geometry(positions, directions, input_order):
    placed = jnp.take(positions, input_order, axis=1)
    geometry = directions[0][:, None] * placed[0][None, :]
    geometry = geometry + directions[1][:, None] * placed[1][None, :]
    return geometry + directions[2][:, None] * placed[2][None, :]


def steering(geometry, gain_row, frequency):
    phases = TWO_PI * frequency * geometry
    cosine = jnp.cos(phases)
    sine_part = jnp.sin(phases)
    weight_norm = 1.0 / math.sqrt(INPUTS)
    w_real = ((gain_row[0] * cosine + gain_row[1] * sine_part) * weight_norm).astype(jnp.bfloat16)
    w_imag = ((gain_row[1] * cosine - gain_row[0] * sine_part) * weight_norm).astype(jnp.bfloat16)
    upper_rows = jnp.concatenate([w_real, -w_imag], axis=1)
    lower_rows = jnp.concatenate([w_imag, w_real], axis=1)
    return jnp.concatenate([upper_rows, lower_rows], axis=0)


def dedisperse(spectrum, delay_part):
    half_bins = TIME // 2
    bin_ids = jnp.arange(1, half_bins + 1, dtype=jnp.int32)
    turn_counts = delay_part[:, :, None] * bin_ids[None, None, :] % TIME
    angles = TWO_PI * turn_counts.astype(jnp.float32) / TIME
    cosine = jnp.cos(angles)
    sine_part = jnp.sin(angles)
    spec_real = spectrum[:, :, :half_bins]
    spec_imag = spectrum[:, :, half_bins:]
    highest = lax.Precision.HIGHEST
    out_real = jnp.einsum(
        "cbk,dck->dbk", spec_real, cosine, precision=highest, preferred_element_type=jnp.float32
    ) - jnp.einsum(
        "cbk,dck->dbk", spec_imag, sine_part, precision=highest, preferred_element_type=jnp.float32
    )
    out_imag = jnp.einsum(
        "cbk,dck->dbk", spec_real, sine_part, precision=highest, preferred_element_type=jnp.float32
    ) + jnp.einsum(
        "cbk,dck->dbk", spec_imag, cosine, precision=highest, preferred_element_type=jnp.float32
    )
    factor = 1.0 / math.sqrt(CH)
    return jnp.concatenate([out_real, out_imag], axis=2) * factor


def plain_device(voltages, gains, positions, directions, input_order, delays, search_beams):
    window = pfb_window()
    folded = fold_frames(voltages, window)
    spectra = jnp.einsum("ks,its->kit", dft_table(), folded, preferred_element_type=jnp.float32)
    spectra = spectra.astype(jnp.bfloat16).reshape(CH, 2, voltages.shape[0], TIME)
    geometry = array_geometry(positions, directions, input_order)
    turned = lax.all_to_all(spectra, "crate", split_axis=0, concat_axis=2, tiled=True)
    local_count = turned.shape[0]
    first_channel = lax.axis_index("crate") * local_count

    def one_channel(packed):
        offsets, channel_data, gain_row = packed
        frequency = 1.0 + (first_channel + offsets).astype(jnp.float32) / CH
        weights = steering(geometry, gain_row, frequency)
        beam_sums = jnp.dot(
            weights,
            channel_data.reshape(2 * INPUTS, channel_data.shape[-1]),
            preferred_element_type=jnp.float32,
        )
        return beam_sums[:BEAMS] * beam_sums[:BEAMS] + beam_sums[BEAMS:] * beam_sums[BEAMS:]

    beam_power = lax.map(one_channel, (jnp.arange(local_count, dtype=jnp.int32), turned, gains))
    local_channels = beam_power.shape[0]
    chosen = jnp.take(beam_power, search_beams, axis=1)
    power_spectra = jnp.dot(
        chosen.reshape(local_channels * SEARCH, TIME),
        time_table(),
        precision=lax.Precision.HIGHEST,
        preferred_element_type=jnp.float32,
    )
    power_spectra = power_spectra.reshape(local_channels, SEARCH, TIME)
    trial_rows = TRIALS // lax.axis_size("crate")
    first_trial = lax.axis_index("crate") * trial_rows
    own_delays = lax.dynamic_slice_in_dim(delays, first_trial, trial_rows, 0)
    dm_plane = dedisperse(lax.all_gather(power_spectra, "crate", axis=0, tiled=True), own_delays)
    return (beam_power, dm_plane)


LANES = 128
MESH = pl.DeviceIdType.MESH


def constant_tables():
    n = np.arange(TAPS * FFTLEN, dtype=np.float64)
    u = (n - 0.5 * TAPS * FFTLEN + 0.5) / FFTLEN
    taper = 0.54 - 0.46 * np.cos(TWO_PI * n / (TAPS * FFTLEN - 1))
    window = (np.sinc(u) * taper).reshape(TAPS, FFTLEN).astype(np.float32)
    c = np.arange(CH)[:, None]
    s = np.arange(FFTLEN)[None, :]
    angles = TWO_PI * (c * s % FFTLEN) / FFTLEN
    table = np.stack([np.cos(angles), -np.sin(angles)], axis=1) / math.sqrt(FFTLEN)
    dft = table.reshape(2 * CH, FFTLEN).astype(jnp.bfloat16)
    t = np.arange(TIME)[:, None]
    k = np.arange(1, TIME // 2 + 1)[None, :]
    turns = TWO_PI * (t * k % TIME) / TIME
    steps = np.concatenate([np.cos(turns), -np.sin(turns)], axis=1) / math.sqrt(TIME * CH)
    spread = np.repeat(steps, SEARCH, axis=1).astype(np.float32)
    return window, dft, spread


def turn(x):
    y = (x - jnp.round(x)) * math.pi
    z = y * y
    sine = 1.0 / math.factorial(11) * -1.0
    for power in (9, 7, 5, 3, 1):
        sine = sine * z + (-1.0) ** (power // 2) / math.factorial(power)
    sine = sine * y
    cosine = 1.0 / math.factorial(12)
    for power in (10, 8, 6, 4, 2, 0):
        cosine = cosine * z + (-1.0) ** (power // 2) / math.factorial(power)
    return 1.0 - 2.0 * sine * sine, 2.0 * sine * cosine


def split_three(x):
    high = x.astype(jnp.bfloat16)
    left = x - high.astype(jnp.float32)
    middle = left.astype(jnp.bfloat16)
    return high, middle, (left - middle.astype(jnp.float32)).astype(jnp.bfloat16)


def crate_kernel(
    n, volts, window, dft, gains, positions, directions, order, delays, beams, spread,
    power, plane,
    folded, frames, sent, held, parts, wheel, sums, twist, onehot, mine, gathered,
    send_sem, recv_sem, own_sem, share_send, share_recv,
):
    me = lax.axis_index("crate")
    rows = 2 * CH // n
    local = CH // n
    trials = TRIALS // n
    half = TIME // 2
    f32, bf16 = jnp.float32, jnp.bfloat16

    def peer(step):
        return lax.rem(me + step, n)

    barrier = pltpu.get_barrier_semaphore()

    def greet(step, carry):
        pl.semaphore_signal(barrier, inc=1, device_id={"crate": peer(step)}, device_id_type=MESH)
        return carry

    lax.fori_loop(1, n, greet, 0)

    def fold(t, carry):
        total = None
        for tap in range(TAPS):
            at = pl.multiple_of((t + tap) * FFTLEN, FFTLEN)
            term = window[tap : tap + 1, :] * volts[:, pl.ds(at, FFTLEN)].astype(f32)
            total = term if total is None else total + term
        folded[t] = total.astype(bf16)
        return carry

    lax.fori_loop(0, TIME, fold, 0)

    def channelize(pair, carry):
        block = folded[pl.ds(2 * pair, 2)].reshape(2 * LANES, FFTLEN)
        out = lax.dot_general(
            dft[...], block, (((1,), (1,)), ((), ())), preferred_element_type=f32
        )
        for which in range(2):
            at = pl.multiple_of((2 * pair + which) * 2 * CH, 2 * CH)
            frames[pl.ds(at, 2 * CH), :] = out[:, which * LANES : (which + 1) * LANES]
        return carry

    lax.fori_loop(0, TIME // 2, channelize, 0)

    def pack(step):
        first = peer(step) * rows
        for row in range(rows):
            sent[step, row] = frames[pl.ds(first + row, TIME, stride=2 * CH), :].astype(bf16)

    def turned(step):
        return pltpu.make_async_remote_copy(
            src_ref=sent.at[step],
            dst_ref=held.at[step],
            send_sem=send_sem.at[step],
            recv_sem=recv_sem.at[step],
            device_id={"crate": peer(step)},
            device_id_type=MESH,
        )

    pl.semaphore_wait(barrier, n - 1)

    def send(step, carry):
        pack(step)
        turned(step).start()
        return carry

    lax.fori_loop(1, n, send, 0)
    pack(0)
    own = pltpu.make_async_copy(sent.at[0], held.at[0], own_sem)
    own.start()

    for index, part in enumerate(split_three(positions[...])):
        parts[index] = part
    beam_ids = lax.broadcasted_iota(jnp.int32, (BEAMS, TIME * SEARCH), 0)
    onehot[...] = jnp.where(beam_ids == beams[...], 1.0, 0.0).astype(bf16)

    at = pl.multiple_of(me * trials, trials)
    cos_one, sin_one = turn(delays[pl.ds(at, trials), :].astype(f32) * (1.0 / TIME))
    cosine, sine = cos_one, sin_one
    for k in range(half):
        low = cosine.astype(bf16)
        high = sine.astype(bf16)
        twist[k, :trials, :CH] = low
        twist[k, :trials, CH:] = -high
        twist[k, trials:, :CH] = high
        twist[k, trials:, CH:] = low
        cosine, sine = cosine * cos_one - sine * sin_one, sine * cos_one + cosine * sin_one

    sums[...] = jnp.zeros_like(sums)
    start = 1.0 + (me * local).astype(f32) * (1.0 / CH)
    own.wait()

    def steer(source):
        at = pl.multiple_of(source * LANES, LANES)
        antenna = lax.broadcasted_iota(jnp.int32, (INPUTS, LANES), 0)
        pick = jnp.where(antenna == order[:, pl.ds(at, LANES)], 1.0, 0.0).astype(bf16)
        placed = None
        for index in range(3):
            term = jnp.dot(parts[index], pick, preferred_element_type=f32)
            placed = term if placed is None else placed + term
        placed = jnp.concatenate([placed] * (LANES // 16), axis=0).T
        columns = BEAMS // 2
        for block in range(LANES // 16):
            p = placed[block * 16 : (block + 1) * 16]
            for side in range(2):
                lanes = slice(side * columns, (side + 1) * columns)
                turns = p[:, 0:1] * directions[0:1, lanes]
                turns = turns + p[:, 1:2] * directions[1:2, lanes]
                turns = turns + p[:, 2:3] * directions[2:3, lanes]
                cosine, sine = turn(turns * start)
                cos_step, sin_step = turn(turns * (1.0 / CH))
                real, imag = cosine, -sine
                for c in range(local):
                    wheel[c, block * 16 : (block + 1) * 16, lanes] = real.astype(bf16)
                    wheel[c, LANES + block * 16 : LANES + (block + 1) * 16, lanes] = imag.astype(bf16)
                    if c + 1 < local:
                        real, imag = (
                            real * cos_step + imag * sin_step,
                            imag * cos_step - real * sin_step,
                        )

    def add_source(step, carry):
        source = lax.rem(me - step + n, n)
        steer(source)

        @pl.when(step > 0)
        def _():
            turned(step).wait_recv()

        at = pl.multiple_of(source * LANES, LANES)

        def add_channel(c, inner):
            gain = gains[c, :, pl.ds(at, LANES)] * (1.0 / math.sqrt(INPUTS))
            gain_real, gain_imag = gain[0:1], gain[1:2]
            real = held[step, 2 * c].astype(f32)
            imag = held[step, 2 * c + 1].astype(f32)
            y_real = (gain_real * real - gain_imag * imag).astype(bf16)
            y_imag = (gain_real * imag + gain_imag * real).astype(bf16)
            left = jnp.concatenate(
                [
                    jnp.concatenate([y_real, -y_imag], axis=1),
                    jnp.concatenate([y_imag, y_real], axis=1),
                ],
                axis=0,
            )
            sums[c] += jnp.dot(left, wheel[c], preferred_element_type=f32)
            return inner

        lax.fori_loop(0, local, add_channel, 0, unroll=4)
        return carry

    lax.fori_loop(0, n, add_source, 0)

    def detect(c, carry):
        total = sums[c]
        power[c] = total[:TIME] * total[:TIME] + total[TIME:] * total[TIME:]
        return carry

    lax.fori_loop(0, local, detect, 0)
    flat = power[...].reshape(local * TIME, BEAMS)
    high = flat.astype(bf16)
    low = (flat - high.astype(f32)).astype(bf16)
    chosen = jnp.dot(high, onehot[...], preferred_element_type=f32) + jnp.dot(
        low, onehot[...], preferred_element_type=f32
    )
    chosen = chosen.reshape(local, TIME, TIME * SEARCH) * spread[...][None]
    mine[...] = jnp.sum(chosen, axis=1).astype(bf16)
    here = pl.ds(pl.multiple_of(me * local, local), local)
    gathered[here, :] = mine[...]

    def shared(step):
        return pltpu.make_async_remote_copy(
            src_ref=mine,
            dst_ref=gathered.at[here],
            send_sem=share_send.at[step],
            recv_sem=share_recv.at[step],
            device_id={"crate": peer(step)},
            device_id_type=MESH,
        )

    def share(step, carry):
        shared(step).start()
        return carry

    def drain(step, carry):
        turned(step).wait_send()
        return carry

    def arrive(step, carry):
        shared(step).wait()
        return carry

    lax.fori_loop(1, n, share, 0)
    lax.fori_loop(1, n, drain, 0)
    lax.fori_loop(1, n, arrive, 0)

    everything = gathered[...]
    right = jnp.concatenate([everything[:, : half * SEARCH], everything[:, half * SEARCH :]], axis=0)
    bins = lax.broadcasted_iota(jnp.int32, (2 * trials, half * SEARCH), 1) // SEARCH
    out = jnp.zeros((2 * trials, half * SEARCH), f32)
    for k in range(half):
        out = jnp.where(bins == k, jnp.dot(twist[k], right, preferred_element_type=f32), out)
    plane[...] = out


def crate_device(n, voltages, gains, positions, directions, input_order, delays, search_beams):
    window, dft, spread = constant_tables()
    local = CH // n
    rows = 2 * local
    trials = TRIALS // n
    half = TIME // 2
    f32, bf16 = jnp.float32, jnp.bfloat16
    vmem = pl.BlockSpec(memory_space=pltpu.VMEM)
    power, plane = pl.pallas_call(
        functools.partial(crate_kernel, n),
        out_shape=(
            jax.ShapeDtypeStruct((local, TIME, BEAMS), f32),
            jax.ShapeDtypeStruct((2 * trials, half * SEARCH), f32),
        ),
        in_specs=[vmem] * 10,
        out_specs=(vmem, vmem),
        scratch_shapes=[
            pltpu.VMEM((TIME, LANES, FFTLEN), bf16),
            pltpu.VMEM((TIME * 2 * CH, LANES), f32),
            pltpu.VMEM((n, rows, TIME, LANES), bf16),
            pltpu.VMEM((n, rows, TIME, LANES), bf16),
            pltpu.VMEM((3, 16, INPUTS), bf16),
            pltpu.VMEM((local, 2 * LANES, BEAMS), bf16),
            pltpu.VMEM((local, 2 * TIME, BEAMS), f32),
            pltpu.VMEM((half, 2 * trials, 2 * CH), bf16),
            pltpu.VMEM((BEAMS, TIME * SEARCH), bf16),
            pltpu.VMEM((local, TIME * SEARCH), bf16),
            pltpu.VMEM((CH, TIME * SEARCH), bf16),
            pltpu.SemaphoreType.DMA((n,)),
            pltpu.SemaphoreType.DMA((n,)),
            pltpu.SemaphoreType.DMA,
            pltpu.SemaphoreType.DMA((n,)),
            pltpu.SemaphoreType.DMA((n,)),
        ],
        compiler_params=pltpu.CompilerParams(
            collective_id=0, has_side_effects=True, vmem_limit_bytes=56 * 1024 * 1024
        ),
    )(
        voltages,
        jnp.asarray(window),
        jnp.asarray(dft),
        gains,
        jnp.pad(positions, ((0, 13), (0, 0))),
        directions,
        input_order[None, :],
        delays,
        jnp.tile(search_beams, TIME)[None, :],
        jnp.asarray(spread),
    )
    plane = plane.reshape(2, trials, half, SEARCH).transpose(1, 3, 0, 2)
    return jnp.swapaxes(power, 1, 2), plane.reshape(trials, SEARCH, TIME)


def solution(mesh):
    in_specs = (P(("groups", "crate"), None), P("crate", None, None), P(), P(), P(), P(), P())
    out_specs = (P(("groups", "crate"), None, None), P(("groups", "crate"), None, None))
    n = mesh.shape["crate"]
    fits = INPUTS // n == LANES and (CH // n) % 16 == 0 and (TRIALS // n) % 16 == 0
    body = functools.partial(crate_device, n) if fits else plain_device
    return jax.shard_map(body, mesh=mesh, in_specs=in_specs, out_specs=out_specs, check_vma=False)
```

```python
import functools
import math

import jax
import jax.numpy as jnp
import numpy as np
from jax import lax
from jax.experimental import pallas as pl
from jax.experimental.pallas import tpu as pltpu
from jax.sharding import PartitionSpec as P

INPUTS = 2048
CH = 256
BEAMS = 512
TRIALS = 1024
TAPS = 4
TIME = 32
SEARCH = 16
FFTLEN = 512


TWO_PI = 2.0 * math.pi


def pfb_window():
    window_len = TAPS * FFTLEN
    sample_index = jnp.arange(window_len, dtype=jnp.int32).astype(jnp.float32)
    offsets = (sample_index - 0.5 * window_len + 0.5) / FFTLEN
    tapering = 0.54 - 0.46 * jnp.cos(TWO_PI * sample_index / (window_len - 1))
    return (jnp.sinc(offsets) * tapering).reshape(TAPS, FFTLEN)


def fold_frames(voltages, window):
    frames = voltages.reshape(voltages.shape[0], TIME + TAPS - 1, FFTLEN)
    summed = window[0] * frames[:, 0:TIME].astype(jnp.float32)
    for tap_index in range(1, TAPS):
        summed = summed + window[tap_index] * frames[:, tap_index : tap_index + TIME].astype(
            jnp.float32
        )
    return summed.astype(jnp.bfloat16)


def dft_table():
    channel_ids = jnp.arange(CH, dtype=jnp.int32)[:, None]
    sample_ids = jnp.arange(FFTLEN, dtype=jnp.int32)[None, :]
    angles = TWO_PI * (channel_ids * sample_ids % FFTLEN).astype(jnp.float32) / FFTLEN
    factor = 1.0 / math.sqrt(FFTLEN)
    stacked = jnp.stack([jnp.cos(angles) * factor, -jnp.sin(angles) * factor], axis=1)
    return stacked.reshape(2 * CH, FFTLEN).astype(jnp.bfloat16)


def time_table():
    step_ids = jnp.arange(TIME, dtype=jnp.int32)[:, None]
    bin_ids = jnp.arange(1, TIME // 2 + 1, dtype=jnp.int32)[None, :]
    angles = TWO_PI * (step_ids * bin_ids % TIME).astype(jnp.float32) / TIME
    factor = 1.0 / math.sqrt(TIME)
    return jnp.concatenate([jnp.cos(angles) * factor, -jnp.sin(angles) * factor], axis=1)


def array_geometry(positions, directions, input_order):
    placed = jnp.take(positions, input_order, axis=1)
    geometry = directions[0][:, None] * placed[0][None, :]
    geometry = geometry + directions[1][:, None] * placed[1][None, :]
    return geometry + directions[2][:, None] * placed[2][None, :]


def steering(geometry, gain_row, frequency):
    phases = TWO_PI * frequency * geometry
    cosine = jnp.cos(phases)
    sine_part = jnp.sin(phases)
    weight_norm = 1.0 / math.sqrt(INPUTS)
    w_real = ((gain_row[0] * cosine + gain_row[1] * sine_part) * weight_norm).astype(jnp.bfloat16)
    w_imag = ((gain_row[1] * cosine - gain_row[0] * sine_part) * weight_norm).astype(jnp.bfloat16)
    upper_rows = jnp.concatenate([w_real, -w_imag], axis=1)
    lower_rows = jnp.concatenate([w_imag, w_real], axis=1)
    return jnp.concatenate([upper_rows, lower_rows], axis=0)


def dedisperse(spectrum, delay_part):
    half_bins = TIME // 2
    bin_ids = jnp.arange(1, half_bins + 1, dtype=jnp.int32)
    turn_counts = delay_part[:, :, None] * bin_ids[None, None, :] % TIME
    angles = TWO_PI * turn_counts.astype(jnp.float32) / TIME
    cosine = jnp.cos(angles)
    sine_part = jnp.sin(angles)
    spec_real = spectrum[:, :, :half_bins]
    spec_imag = spectrum[:, :, half_bins:]
    highest = lax.Precision.HIGHEST
    out_real = jnp.einsum(
        "cbk,dck->dbk", spec_real, cosine, precision=highest, preferred_element_type=jnp.float32
    ) - jnp.einsum(
        "cbk,dck->dbk", spec_imag, sine_part, precision=highest, preferred_element_type=jnp.float32
    )
    out_imag = jnp.einsum(
        "cbk,dck->dbk", spec_real, sine_part, precision=highest, preferred_element_type=jnp.float32
    ) + jnp.einsum(
        "cbk,dck->dbk", spec_imag, cosine, precision=highest, preferred_element_type=jnp.float32
    )
    factor = 1.0 / math.sqrt(CH)
    return jnp.concatenate([out_real, out_imag], axis=2) * factor


def plain_device(voltages, gains, positions, directions, input_order, delays, search_beams):
    window = pfb_window()
    folded = fold_frames(voltages, window)
    spectra = jnp.einsum("ks,its->kit", dft_table(), folded, preferred_element_type=jnp.float32)
    spectra = spectra.astype(jnp.bfloat16).reshape(CH, 2, voltages.shape[0], TIME)
    geometry = array_geometry(positions, directions, input_order)
    turned = lax.all_to_all(spectra, "crate", split_axis=0, concat_axis=2, tiled=True)
    local_count = turned.shape[0]
    first_channel = lax.axis_index("crate") * local_count

    def one_channel(packed):
        offsets, channel_data, gain_row = packed
        frequency = 1.0 + (first_channel + offsets).astype(jnp.float32) / CH
        weights = steering(geometry, gain_row, frequency)
        beam_sums = jnp.dot(
            weights,
            channel_data.reshape(2 * INPUTS, channel_data.shape[-1]),
            preferred_element_type=jnp.float32,
        )
        return beam_sums[:BEAMS] * beam_sums[:BEAMS] + beam_sums[BEAMS:] * beam_sums[BEAMS:]

    beam_power = lax.map(one_channel, (jnp.arange(local_count, dtype=jnp.int32), turned, gains))
    local_channels = beam_power.shape[0]
    chosen = jnp.take(beam_power, search_beams, axis=1)
    power_spectra = jnp.dot(
        chosen.reshape(local_channels * SEARCH, TIME),
        time_table(),
        precision=lax.Precision.HIGHEST,
        preferred_element_type=jnp.float32,
    )
    power_spectra = power_spectra.reshape(local_channels, SEARCH, TIME)
    trial_rows = TRIALS // lax.axis_size("crate")
    first_trial = lax.axis_index("crate") * trial_rows
    own_delays = lax.dynamic_slice_in_dim(delays, first_trial, trial_rows, 0)
    dm_plane = dedisperse(lax.all_gather(power_spectra, "crate", axis=0, tiled=True), own_delays)
    return (beam_power, dm_plane)


LANES = 128
MESH = pl.DeviceIdType.MESH


def constant_tables():
    n = np.arange(TAPS * FFTLEN, dtype=np.float64)
    u = (n - 0.5 * TAPS * FFTLEN + 0.5) / FFTLEN
    taper = 0.54 - 0.46 * np.cos(TWO_PI * n / (TAPS * FFTLEN - 1))
    window = (np.sinc(u) * taper).reshape(TAPS, FFTLEN).astype(np.float32)
    c = np.arange(CH)[:, None]
    s = np.arange(FFTLEN)[None, :]
    angles = TWO_PI * (c * s % FFTLEN) / FFTLEN
    table = np.stack([np.cos(angles), -np.sin(angles)], axis=1) / math.sqrt(FFTLEN)
    dft = table.reshape(2 * CH, FFTLEN).astype(np.float32)
    t = np.arange(TIME)[:, None]
    k = np.arange(1, TIME // 2 + 1)[None, :]
    turns = TWO_PI * (t * k % TIME) / TIME
    steps = np.concatenate([np.cos(turns), -np.sin(turns)], axis=1) / math.sqrt(TIME * CH)
    spread = np.concatenate(
        [np.tile(steps[:, : TIME // 2], (1, SEARCH)), np.tile(steps[:, TIME // 2 :], (1, SEARCH))],
        axis=1,
    ).astype(np.float32)
    return window, dft, spread


def turn(x):
    y = (x - jnp.round(x)) * math.pi
    z = y * y
    sine = 1.0 / math.factorial(11) * -1.0
    for power in (9, 7, 5, 3, 1):
        sine = sine * z + (-1.0) ** (power // 2) / math.factorial(power)
    sine = sine * y
    cosine = 1.0 / math.factorial(12)
    for power in (10, 8, 6, 4, 2, 0):
        cosine = cosine * z + (-1.0) ** (power // 2) / math.factorial(power)
    return 1.0 - 2.0 * sine * sine, 2.0 * sine * cosine


def split_three(x):
    high = x.astype(jnp.bfloat16)
    left = x - high.astype(jnp.float32)
    middle = left.astype(jnp.bfloat16)
    return high, middle, (left - middle.astype(jnp.float32)).astype(jnp.bfloat16)


def crate_kernel(
    n, volts, window, dft, gains, positions, directions, order, delays, beams, spread,
    power, plane,
    table, frames, sent, held, parts, columns, wheel, sums, twist, onehot, mine, gathered,
    send_sem, recv_sem, own_sem, share_send, share_recv,
):
    me = lax.axis_index("crate")
    rows = 2 * CH // n
    local = CH // n
    trials = TRIALS // n
    half = TIME // 2
    f32, bf16 = jnp.float32, jnp.bfloat16

    def peer(step):
        return lax.rem(me + step, n)

    barrier = pltpu.get_barrier_semaphore()

    def greet(step, carry):
        pl.semaphore_signal(barrier, inc=1, device_id={"crate": peer(step)}, device_id_type=MESH)
        return carry

    lax.fori_loop(1, n, greet, 0)

    table[...] = dft[...].astype(bf16)

    def fold(t):
        total = None
        for tap in range(TAPS):
            at = pl.multiple_of((t + tap) * FFTLEN, FFTLEN)
            term = window[tap : tap + 1, :] * volts[:, pl.ds(at, FFTLEN)].astype(f32)
            total = term if total is None else total + term
        return total.astype(bf16)

    def channelize(pair, carry):
        block = jnp.concatenate([fold(2 * pair), fold(2 * pair + 1)], axis=0)
        out = lax.dot_general(
            table[...], block, (((1,), (1,)), ((), ())), preferred_element_type=f32
        )
        for which in range(2):
            at = pl.multiple_of((2 * pair + which) * 2 * CH, 2 * CH)
            frames[pl.ds(at, 2 * CH), :] = out[:, which * LANES : (which + 1) * LANES]
        return carry

    lax.fori_loop(0, TIME // 2, channelize, 0, unroll=2)

    def pack(step):
        first = peer(step) * rows
        for row in range(rows):
            sent[step, row] = frames[pl.ds(first + row, TIME, stride=2 * CH), :].astype(bf16)

    def turned(step):
        return pltpu.make_async_remote_copy(
            src_ref=sent.at[step],
            dst_ref=held.at[step],
            send_sem=send_sem.at[step],
            recv_sem=recv_sem.at[step],
            device_id={"crate": peer(step)},
            device_id_type=MESH,
        )

    pl.semaphore_wait(barrier, n - 1)

    def send(step, carry):
        pack(step)
        turned(step).start()
        return carry

    lax.fori_loop(1, n, send, 0)
    pack(0)
    own = pltpu.make_async_copy(sent.at[0], held.at[0], own_sem)
    own.start()

    parts[...] = jnp.zeros_like(parts)
    for index, part in enumerate(split_three(positions[...])):
        parts[16 * index : 16 * index + 3] = part
    beam_ids = lax.broadcasted_iota(jnp.int32, (BEAMS, SEARCH), 0)
    listed = jnp.where(beam_ids == beams[...], 1.0, 0.0).astype(bf16)
    search_ids = lax.broadcasted_iota(jnp.int32, (SEARCH, TIME * SEARCH), 0)
    lane_ids = lax.broadcasted_iota(jnp.int32, (SEARCH, TIME * SEARCH), 1)
    widen = jnp.where(lane_ids // half % SEARCH == search_ids, 1.0, 0.0).astype(bf16)
    onehot[...] = jnp.dot(listed, widen, preferred_element_type=f32).astype(bf16)

    at = pl.multiple_of(me * trials, trials)
    cos_one, sin_one = turn(delays[pl.ds(at, trials), :].astype(f32) * (1.0 / TIME))
    cosine, sine = cos_one, sin_one
    for k in range(half):
        low = cosine.astype(bf16)
        high = sine.astype(bf16)
        twist[k, :trials, :CH] = low
        twist[k, :trials, CH:] = -high
        twist[k, trials:, :CH] = high
        twist[k, trials:, CH:] = low
        cosine, sine = cosine * cos_one - sine * sin_one, sine * cos_one + cosine * sin_one

    sums[...] = jnp.zeros_like(sums)
    start = 1.0 + (me * local).astype(f32) * (1.0 / CH)
    own.wait()

    def place(source):
        at = pl.multiple_of(source * LANES, LANES)
        antenna = lax.broadcasted_iota(jnp.int32, (INPUTS, LANES), 0)
        pick = jnp.where(antenna == order[:, pl.ds(at, LANES)], 1.0, 0.0).astype(bf16)
        out = jnp.dot(parts[...], pick, preferred_element_type=f32)
        placed = out[0:16] + out[16:32] + out[32:48]
        columns[...] = jnp.concatenate([placed] * (LANES // 16), axis=0).T

    def steer(block, slot):
        first = pl.multiple_of(block * 16, 16)
        p = columns[pl.ds(first, 16), :]
        width = BEAMS // 2
        for side in range(2):
            lanes = slice(side * width, (side + 1) * width)
            turns = p[:, 0:1] * directions[0:1, lanes]
            turns = turns + p[:, 1:2] * directions[1:2, lanes]
            turns = turns + p[:, 2:3] * directions[2:3, lanes]
            cosine, sine = turn(turns * start)
            cos_step, sin_step = turn(turns * (1.0 / CH))
            real, imag = cosine, -sine
            ahead = (real * cos_step + imag * sin_step, imag * cos_step - real * sin_step)
            twice = 2.0 * cos_step
            for c in range(local):
                wheel[slot, c, pl.ds(first, 16), lanes] = real.astype(bf16)
                wheel[slot, c, pl.ds(LANES + first, 16), lanes] = imag.astype(bf16)
                if c + 1 < local:
                    after = (twice * ahead[0] - real, twice * ahead[1] - imag)
                    (real, imag), ahead = ahead, after

    def add_channel(c, step, slot, at):
        gain = gains[c, :, pl.ds(at, LANES)] * (1.0 / math.sqrt(INPUTS))
        gain_real, gain_imag = gain[0:1], gain[1:2]
        real = held[step, 2 * c].astype(f32)
        imag = held[step, 2 * c + 1].astype(f32)
        y_real = (gain_real * real - gain_imag * imag).astype(bf16)
        y_imag = (gain_real * imag + gain_imag * real).astype(bf16)
        left = jnp.concatenate(
            [
                jnp.concatenate([y_real, -y_imag], axis=1),
                jnp.concatenate([y_imag, y_real], axis=1),
            ],
            axis=0,
        )
        sums[c] += jnp.dot(left, wheel[slot, c], preferred_element_type=f32)

    blocks = LANES // 16
    per_block = local // blocks

    def owner(step):
        return lax.rem(me - step + n, n)

    def add_source(step, steering_on):
        slot = lax.rem(step, 2)
        at = pl.multiple_of(owner(step) * LANES, LANES)
        if steering_on:
            place(owner(step + 1))

        def body(block, carry):
            if steering_on:
                steer(block, 1 - slot)
            for c in range(per_block):
                add_channel(block * per_block + c, step, slot, at)
            return carry

        lax.fori_loop(0, blocks, body, 0, unroll=1 if steering_on else 4)

    def first_steer(block, carry):
        steer(block, 0)
        return carry

    place(me)
    lax.fori_loop(0, blocks, first_steer, 0)

    def middle(step, carry):
        @pl.when(step > 0)
        def _():
            turned(step).wait_recv()

        add_source(step, True)
        return carry

    lax.fori_loop(0, n - 1, middle, 0)
    turned(n - 1).wait_recv()
    add_source(n - 1, False)

    def detect(c, carry):
        total = sums[c]
        power[c] = total[:TIME] * total[:TIME] + total[TIME:] * total[TIME:]
        return carry

    lax.fori_loop(0, local, detect, 0)
    flat = power[...].reshape(local * TIME, BEAMS)
    high = flat.astype(bf16)
    low = (flat - high.astype(f32)).astype(bf16)
    chosen = jnp.dot(high, onehot[...], preferred_element_type=f32) + jnp.dot(
        low, onehot[...], preferred_element_type=f32
    )
    chosen = chosen.reshape(local, TIME, TIME * SEARCH) * spread[...][None]
    mine[...] = jnp.sum(chosen, axis=1).astype(bf16)
    here = pl.ds(pl.multiple_of(me * local, local), local)
    gathered[here, :] = mine[...]

    def shared(step):
        return pltpu.make_async_remote_copy(
            src_ref=mine,
            dst_ref=gathered.at[here],
            send_sem=share_send.at[step],
            recv_sem=share_recv.at[step],
            device_id={"crate": peer(step)},
            device_id_type=MESH,
        )

    def share(step, carry):
        shared(step).start()
        return carry

    def drain(step, carry):
        turned(step).wait_send()
        return carry

    def arrive(step, carry):
        shared(step).wait()
        return carry

    lax.fori_loop(1, n, share, 0)
    lax.fori_loop(1, n, drain, 0)
    lax.fori_loop(1, n, arrive, 0)

    everything = gathered[...]
    right = jnp.concatenate([everything[:, : half * SEARCH], everything[:, half * SEARCH :]], axis=0)
    bins = lax.broadcasted_iota(jnp.int32, (2 * trials, half * SEARCH), 1) % half
    out = jnp.zeros((2 * trials, half * SEARCH), f32)
    for k in range(half):
        out = jnp.where(bins == k, jnp.dot(twist[k], right, preferred_element_type=f32), out)
    out = out.T.reshape(SEARCH, half, 2 * trials)
    plane[:, :half, :] = out[:, :, :trials]
    plane[:, half:, :] = out[:, :, trials:]


def crate_device(n, voltages, gains, positions, directions, input_order, delays, search_beams):
    window, dft, spread = constant_tables()
    local = CH // n
    rows = 2 * local
    trials = TRIALS // n
    half = TIME // 2
    f32, bf16 = jnp.float32, jnp.bfloat16
    vmem = pl.BlockSpec(memory_space=pltpu.VMEM)
    power, plane = pl.pallas_call(
        functools.partial(crate_kernel, n),
        out_shape=(
            jax.ShapeDtypeStruct((local, TIME, BEAMS), f32),
            jax.ShapeDtypeStruct((SEARCH, TIME, trials), f32),
        ),
        in_specs=[vmem] * 10,
        out_specs=(vmem, vmem),
        scratch_shapes=[
            pltpu.VMEM((2 * CH, FFTLEN), bf16),
            pltpu.VMEM((TIME * 2 * CH, LANES), f32),
            pltpu.VMEM((n, rows, TIME, LANES), bf16),
            pltpu.VMEM((n, rows, TIME, LANES), bf16),
            pltpu.VMEM((48, INPUTS), bf16),
            pltpu.VMEM((LANES, LANES), f32),
            pltpu.VMEM((2, local, 2 * LANES, BEAMS), bf16),
            pltpu.VMEM((local, 2 * TIME, BEAMS), f32),
            pltpu.VMEM((half, 2 * trials, 2 * CH), bf16),
            pltpu.VMEM((BEAMS, TIME * SEARCH), bf16),
            pltpu.VMEM((local, TIME * SEARCH), bf16),
            pltpu.VMEM((CH, TIME * SEARCH), bf16),
            pltpu.SemaphoreType.DMA((n,)),
            pltpu.SemaphoreType.DMA((n,)),
            pltpu.SemaphoreType.DMA,
            pltpu.SemaphoreType.DMA((n,)),
            pltpu.SemaphoreType.DMA((n,)),
        ],
        compiler_params=pltpu.CompilerParams(
            collective_id=0, has_side_effects=True, vmem_limit_bytes=56 * 1024 * 1024
        ),
    )(
        voltages,
        jnp.asarray(window),
        jnp.asarray(dft),
        gains,
        positions,
        directions,
        input_order[None, :],
        delays,
        search_beams[None, :],
        jnp.asarray(spread),
    )
    return jnp.swapaxes(power, 1, 2), plane.transpose(2, 0, 1)


def solution(mesh):
    in_specs = (P(("groups", "crate"), None), P("crate", None, None), P(), P(), P(), P(), P())
    out_specs = (P(("groups", "crate"), None, None), P(("groups", "crate"), None, None))
    n = mesh.shape["crate"]
    fits = INPUTS // n == LANES and (CH // n) % 16 == 0 and (TRIALS // n) % 16 == 0
    body = functools.partial(crate_device, n) if fits else plain_device
    return jax.shard_map(body, mesh=mesh, in_specs=in_specs, out_specs=out_specs, check_vma=False)
```

```python
import functools
import math

import jax
import jax.numpy as jnp
import numpy as np
from jax import lax
from jax.experimental import pallas as pl
from jax.experimental.pallas import tpu as pltpu
from jax.sharding import PartitionSpec as P

INPUTS = 2048
CH = 256
BEAMS = 512
TRIALS = 1024
TAPS = 4
TIME = 32
SEARCH = 16
FFTLEN = 512


TWO_PI = 2.0 * math.pi


def pfb_window():
    window_len = TAPS * FFTLEN
    sample_index = jnp.arange(window_len, dtype=jnp.int32).astype(jnp.float32)
    offsets = (sample_index - 0.5 * window_len + 0.5) / FFTLEN
    tapering = 0.54 - 0.46 * jnp.cos(TWO_PI * sample_index / (window_len - 1))
    return (jnp.sinc(offsets) * tapering).reshape(TAPS, FFTLEN)


def fold_frames(voltages, window):
    frames = voltages.reshape(voltages.shape[0], TIME + TAPS - 1, FFTLEN)
    summed = window[0] * frames[:, 0:TIME].astype(jnp.float32)
    for tap_index in range(1, TAPS):
        summed = summed + window[tap_index] * frames[:, tap_index : tap_index + TIME].astype(
            jnp.float32
        )
    return summed.astype(jnp.bfloat16)


def dft_table():
    channel_ids = jnp.arange(CH, dtype=jnp.int32)[:, None]
    sample_ids = jnp.arange(FFTLEN, dtype=jnp.int32)[None, :]
    angles = TWO_PI * (channel_ids * sample_ids % FFTLEN).astype(jnp.float32) / FFTLEN
    factor = 1.0 / math.sqrt(FFTLEN)
    stacked = jnp.stack([jnp.cos(angles) * factor, -jnp.sin(angles) * factor], axis=1)
    return stacked.reshape(2 * CH, FFTLEN).astype(jnp.bfloat16)


def time_table():
    step_ids = jnp.arange(TIME, dtype=jnp.int32)[:, None]
    bin_ids = jnp.arange(1, TIME // 2 + 1, dtype=jnp.int32)[None, :]
    angles = TWO_PI * (step_ids * bin_ids % TIME).astype(jnp.float32) / TIME
    factor = 1.0 / math.sqrt(TIME)
    return jnp.concatenate([jnp.cos(angles) * factor, -jnp.sin(angles) * factor], axis=1)


def array_geometry(positions, directions, input_order):
    placed = jnp.take(positions, input_order, axis=1)
    geometry = directions[0][:, None] * placed[0][None, :]
    geometry = geometry + directions[1][:, None] * placed[1][None, :]
    return geometry + directions[2][:, None] * placed[2][None, :]


def steering(geometry, gain_row, frequency):
    phases = TWO_PI * frequency * geometry
    cosine = jnp.cos(phases)
    sine_part = jnp.sin(phases)
    weight_norm = 1.0 / math.sqrt(INPUTS)
    w_real = ((gain_row[0] * cosine + gain_row[1] * sine_part) * weight_norm).astype(jnp.bfloat16)
    w_imag = ((gain_row[1] * cosine - gain_row[0] * sine_part) * weight_norm).astype(jnp.bfloat16)
    upper_rows = jnp.concatenate([w_real, -w_imag], axis=1)
    lower_rows = jnp.concatenate([w_imag, w_real], axis=1)
    return jnp.concatenate([upper_rows, lower_rows], axis=0)


def dedisperse(spectrum, delay_part):
    half_bins = TIME // 2
    bin_ids = jnp.arange(1, half_bins + 1, dtype=jnp.int32)
    turn_counts = delay_part[:, :, None] * bin_ids[None, None, :] % TIME
    angles = TWO_PI * turn_counts.astype(jnp.float32) / TIME
    cosine = jnp.cos(angles)
    sine_part = jnp.sin(angles)
    spec_real = spectrum[:, :, :half_bins]
    spec_imag = spectrum[:, :, half_bins:]
    highest = lax.Precision.HIGHEST
    out_real = jnp.einsum(
        "cbk,dck->dbk", spec_real, cosine, precision=highest, preferred_element_type=jnp.float32
    ) - jnp.einsum(
        "cbk,dck->dbk", spec_imag, sine_part, precision=highest, preferred_element_type=jnp.float32
    )
    out_imag = jnp.einsum(
        "cbk,dck->dbk", spec_real, sine_part, precision=highest, preferred_element_type=jnp.float32
    ) + jnp.einsum(
        "cbk,dck->dbk", spec_imag, cosine, precision=highest, preferred_element_type=jnp.float32
    )
    factor = 1.0 / math.sqrt(CH)
    return jnp.concatenate([out_real, out_imag], axis=2) * factor


def plain_device(voltages, gains, positions, directions, input_order, delays, search_beams):
    window = pfb_window()
    folded = fold_frames(voltages, window)
    spectra = jnp.einsum("ks,its->kit", dft_table(), folded, preferred_element_type=jnp.float32)
    spectra = spectra.astype(jnp.bfloat16).reshape(CH, 2, voltages.shape[0], TIME)
    geometry = array_geometry(positions, directions, input_order)
    turned = lax.all_to_all(spectra, "crate", split_axis=0, concat_axis=2, tiled=True)
    local_count = turned.shape[0]
    first_channel = lax.axis_index("crate") * local_count

    def one_channel(packed):
        offsets, channel_data, gain_row = packed
        frequency = 1.0 + (first_channel + offsets).astype(jnp.float32) / CH
        weights = steering(geometry, gain_row, frequency)
        beam_sums = jnp.dot(
            weights,
            channel_data.reshape(2 * INPUTS, channel_data.shape[-1]),
            preferred_element_type=jnp.float32,
        )
        return beam_sums[:BEAMS] * beam_sums[:BEAMS] + beam_sums[BEAMS:] * beam_sums[BEAMS:]

    beam_power = lax.map(one_channel, (jnp.arange(local_count, dtype=jnp.int32), turned, gains))
    local_channels = beam_power.shape[0]
    chosen = jnp.take(beam_power, search_beams, axis=1)
    power_spectra = jnp.dot(
        chosen.reshape(local_channels * SEARCH, TIME),
        time_table(),
        precision=lax.Precision.HIGHEST,
        preferred_element_type=jnp.float32,
    )
    power_spectra = power_spectra.reshape(local_channels, SEARCH, TIME)
    trial_rows = TRIALS // lax.axis_size("crate")
    first_trial = lax.axis_index("crate") * trial_rows
    own_delays = lax.dynamic_slice_in_dim(delays, first_trial, trial_rows, 0)
    dm_plane = dedisperse(lax.all_gather(power_spectra, "crate", axis=0, tiled=True), own_delays)
    return (beam_power, dm_plane)


LANES = 128
MESH = pl.DeviceIdType.MESH


def constant_tables():
    n = np.arange(TAPS * FFTLEN, dtype=np.float64)
    u = (n - 0.5 * TAPS * FFTLEN + 0.5) / FFTLEN
    taper = 0.54 - 0.46 * np.cos(TWO_PI * n / (TAPS * FFTLEN - 1))
    window = (np.sinc(u) * taper).reshape(TAPS, FFTLEN).astype(np.float32)
    c = np.arange(CH)[:, None]
    s = np.arange(FFTLEN)[None, :]
    angles = TWO_PI * (c * s % FFTLEN) / FFTLEN
    table = np.stack([np.cos(angles), -np.sin(angles)], axis=1) / math.sqrt(FFTLEN)
    dft = table.reshape(2 * CH, FFTLEN).astype(np.float32)
    t = np.arange(TIME)[:, None]
    k = np.arange(1, TIME // 2 + 1)[None, :]
    turns = TWO_PI * (t * k % TIME) / TIME
    steps = np.concatenate([np.cos(turns), -np.sin(turns)], axis=1) / math.sqrt(TIME * CH)
    spread = np.concatenate(
        [np.tile(steps[:, : TIME // 2], (1, SEARCH)), np.tile(steps[:, TIME // 2 :], (1, SEARCH))],
        axis=1,
    ).astype(np.float32)
    return window, dft, spread


def turn(x):
    y = (x - jnp.round(x)) * math.pi
    z = y * y
    sine = 1.0 / math.factorial(11) * -1.0
    for power in (9, 7, 5, 3, 1):
        sine = sine * z + (-1.0) ** (power // 2) / math.factorial(power)
    sine = sine * y
    cosine = 1.0 / math.factorial(12)
    for power in (10, 8, 6, 4, 2, 0):
        cosine = cosine * z + (-1.0) ** (power // 2) / math.factorial(power)
    return 1.0 - 2.0 * sine * sine, 2.0 * sine * cosine


def split_three(x):
    high = x.astype(jnp.bfloat16)
    left = x - high.astype(jnp.float32)
    middle = left.astype(jnp.bfloat16)
    return high, middle, (left - middle.astype(jnp.float32)).astype(jnp.bfloat16)


def crate_kernel(
    n, volts, window, dft, gains, positions, directions, order, delays, beams, spread,
    power, plane,
    table, frames, sent, held, parts, columns, wheel, sums, twist, onehot, mine, gathered,
    lent, leaving, landing,
    send_sem, recv_sem, own_sem, share_send, share_recv, lend_sem, part_send, part_recv,
):
    me = lax.axis_index("crate")
    rows = 2 * CH // n
    local = CH // n
    trials = TRIALS // n
    half = TIME // 2
    f32, bf16 = jnp.float32, jnp.bfloat16

    m = n // 2
    side = me // m
    place_in = lax.rem(me, m)
    twin = (1 - side) * m + place_in

    def peer(step):
        return lax.rem(me + step, n)

    def near(u):
        return side * m + lax.rem(place_in + u, m)

    def owner(u):
        return side * m + lax.rem(place_in - u + 2 * m, m)

    def channel_side(u):
        return side + (1 - u // m) * (1 - 2 * side)

    barrier = pltpu.get_barrier_semaphore()

    def greet(step, carry):
        pl.semaphore_signal(barrier, inc=1, device_id={"crate": peer(step)}, device_id_type=MESH)
        return carry

    lax.fori_loop(1, n, greet, 0)

    table[...] = dft[...].astype(bf16)

    def fold(t):
        total = None
        for tap in range(TAPS):
            at = pl.multiple_of((t + tap) * FFTLEN, FFTLEN)
            term = window[tap : tap + 1, :] * volts[:, pl.ds(at, FFTLEN)].astype(f32)
            total = term if total is None else total + term
        return total.astype(bf16)

    def channelize(pair, carry):
        block = jnp.concatenate([fold(2 * pair), fold(2 * pair + 1)], axis=0)
        out = lax.dot_general(
            table[...], block, (((1,), (1,)), ((), ())), preferred_element_type=f32
        )
        for which in range(2):
            at = pl.multiple_of((2 * pair + which) * 2 * CH, 2 * CH)
            frames[pl.ds(at, 2 * CH), :] = out[:, which * LANES : (which + 1) * LANES]
        return carry

    lax.fori_loop(0, TIME // 2, channelize, 0, unroll=2)

    def pack(u):
        first = (channel_side(u) * m + lax.rem(place_in + u, m)) * rows
        for row in range(rows):
            sent[u, row] = frames[pl.ds(first + row, TIME, stride=2 * CH), :].astype(bf16)

    def turned(u):
        return pltpu.make_async_remote_copy(
            src_ref=sent.at[u],
            dst_ref=held.at[u],
            send_sem=send_sem.at[u],
            recv_sem=recv_sem.at[u],
            device_id={"crate": near(u)},
            device_id_type=MESH,
        )

    def partial(c):
        return pltpu.make_async_remote_copy(
            src_ref=leaving.at[c],
            dst_ref=landing.at[c],
            send_sem=part_send.at[c],
            recv_sem=part_recv.at[c],
            device_id={"crate": twin},
            device_id_type=MESH,
        )

    far = pl.ds(pl.multiple_of((1 - side) * (m * LANES), LANES), m * LANES)
    lend = pltpu.make_async_remote_copy(
        src_ref=gains.at[:, :, far],
        dst_ref=lent,
        send_sem=lend_sem.at[0],
        recv_sem=lend_sem.at[1],
        device_id={"crate": twin},
        device_id_type=MESH,
    )
    pl.semaphore_wait(barrier, n - 1)
    lend.start()

    def send(u, carry):
        pack(u)
        turned(u).start()
        return carry

    lax.fori_loop(1, m, send, 0)
    pack(0)
    own_first = pltpu.make_async_copy(sent.at[0], held.at[0], own_sem.at[0])
    own_first.start()
    lax.fori_loop(m + 1, n, send, 0)
    pack(m)
    own_later = pltpu.make_async_copy(sent.at[m], held.at[m], own_sem.at[1])
    own_later.start()

    parts[...] = jnp.zeros_like(parts)
    for index, part in enumerate(split_three(positions[...])):
        parts[16 * index : 16 * index + 3] = part
    beam_ids = lax.broadcasted_iota(jnp.int32, (BEAMS, SEARCH), 0)
    listed = jnp.where(beam_ids == beams[...], 1.0, 0.0).astype(bf16)
    search_ids = lax.broadcasted_iota(jnp.int32, (SEARCH, TIME * SEARCH), 0)
    lane_ids = lax.broadcasted_iota(jnp.int32, (SEARCH, TIME * SEARCH), 1)
    widen = jnp.where(lane_ids // half % SEARCH == search_ids, 1.0, 0.0).astype(bf16)
    onehot[...] = jnp.dot(listed, widen, preferred_element_type=f32).astype(bf16)

    at = pl.multiple_of(me * trials, trials)
    cos_one, sin_one = turn(delays[pl.ds(at, trials), :].astype(f32) * (1.0 / TIME))
    cosine, sine = cos_one, sin_one
    for k in range(half):
        low = cosine.astype(bf16)
        high = sine.astype(bf16)
        twist[k, :trials, :CH] = low
        twist[k, :trials, CH:] = -high
        twist[k, trials:, :CH] = high
        twist[k, trials:, CH:] = low
        cosine, sine = cosine * cos_one - sine * sin_one, sine * cos_one + cosine * sin_one

    sums[...] = jnp.zeros_like(sums)
    own_first.wait()
    own_later.wait()

    def place(source):
        at = pl.multiple_of(source * LANES, LANES)
        antenna = lax.broadcasted_iota(jnp.int32, (INPUTS, LANES), 0)
        pick = jnp.where(antenna == order[:, pl.ds(at, LANES)], 1.0, 0.0).astype(bf16)
        out = jnp.dot(parts[...], pick, preferred_element_type=f32)
        placed = out[0:16] + out[16:32] + out[32:48]
        columns[...] = jnp.concatenate([placed] * (LANES // 16), axis=0).T

    def steer(block, slot, u):
        first_channel = (channel_side(u) * m + place_in) * local
        start = 1.0 + first_channel.astype(f32) * (1.0 / CH)
        first = pl.multiple_of(block * 16, 16)
        p = columns[pl.ds(first, 16), :]
        width = BEAMS // 2
        for side in range(2):
            lanes = slice(side * width, (side + 1) * width)
            turns = p[:, 0:1] * directions[0:1, lanes]
            turns = turns + p[:, 1:2] * directions[1:2, lanes]
            turns = turns + p[:, 2:3] * directions[2:3, lanes]
            cosine, sine = turn(turns * start)
            cos_step, sin_step = turn(turns * (1.0 / CH))
            real, imag = cosine, -sine
            ahead = (real * cos_step + imag * sin_step, imag * cos_step - real * sin_step)
            twice = 2.0 * cos_step
            for c in range(local):
                wheel[slot, c, pl.ds(first, 16), lanes] = real.astype(bf16)
                wheel[slot, c, pl.ds(LANES + first, 16), lanes] = imag.astype(bf16)
                if c + 1 < local:
                    after = (twice * ahead[0] - real, twice * ahead[1] - imag)
                    (real, imag), ahead = ahead, after

    def add_channel(c, step, slot, gain_ref, at):
        gain = gain_ref[c, :, pl.ds(at, LANES)] * (1.0 / math.sqrt(INPUTS))
        gain_real, gain_imag = gain[0:1], gain[1:2]
        real = held[step, 2 * c].astype(f32)
        imag = held[step, 2 * c + 1].astype(f32)
        y_real = (gain_real * real - gain_imag * imag).astype(bf16)
        y_imag = (gain_real * imag + gain_imag * real).astype(bf16)
        left = jnp.concatenate(
            [
                jnp.concatenate([y_real, -y_imag], axis=1),
                jnp.concatenate([y_imag, y_real], axis=1),
            ],
            axis=0,
        )
        sums[c] += jnp.dot(left, wheel[slot, c], preferred_element_type=f32)

    blocks = LANES // 16
    per_block = local // blocks

    def add_source(u, later, steering_on):
        slot = lax.rem(u, 2)
        gain_ref = gains if later else lent
        source = owner(u) if later else owner(u) - side * m
        at = pl.multiple_of(source * LANES, LANES)
        if steering_on:
            place(owner(u + 1))

        def body(block, carry):
            if steering_on:
                steer(block, 1 - slot, u + 1)
            for c in range(per_block):
                add_channel(block * per_block + c, u, slot, gain_ref, at)
            return carry

        lax.fori_loop(0, blocks, body, 0, unroll=1 if steering_on else 4)

    def first_steer(block, carry):
        steer(block, 0, 0)
        return carry

    place(me)
    lax.fori_loop(0, blocks, first_steer, 0)
    lend.wait()
    add_source(0, False, True)

    def for_twin(u, carry):
        turned(u).wait_recv()
        add_source(u, False, True)
        return carry

    lax.fori_loop(1, m, for_twin, 0)

    def hand_over(c, carry):
        leaving[c] = sums[c].astype(bf16)
        partial(c).start()
        sums[c] = jnp.zeros((2 * TIME, BEAMS), f32)
        return carry

    lax.fori_loop(0, local, hand_over, 0)
    add_source(m, True, True)

    def for_self(u, carry):
        turned(u).wait_recv()
        add_source(u, True, True)
        return carry

    lax.fori_loop(m + 1, n - 1, for_self, 0)
    turned(n - 1).wait_recv()
    add_source(n - 1, True, False)

    def detect(c, carry):
        partial(c).wait()
        total = sums[c] + landing[c].astype(f32)
        power[c] = total[:TIME] * total[:TIME] + total[TIME:] * total[TIME:]
        return carry

    lax.fori_loop(0, local, detect, 0)
    flat = power[...].reshape(local * TIME, BEAMS)
    high = flat.astype(bf16)
    low = (flat - high.astype(f32)).astype(bf16)
    chosen = jnp.dot(high, onehot[...], preferred_element_type=f32) + jnp.dot(
        low, onehot[...], preferred_element_type=f32
    )
    chosen = chosen.reshape(local, TIME, TIME * SEARCH) * spread[...][None]
    mine[...] = jnp.sum(chosen, axis=1).astype(bf16)
    here = pl.ds(pl.multiple_of(me * local, local), local)
    gathered[here, :] = mine[...]

    def shared(step):
        return pltpu.make_async_remote_copy(
            src_ref=mine,
            dst_ref=gathered.at[here],
            send_sem=share_send.at[step],
            recv_sem=share_recv.at[step],
            device_id={"crate": peer(step)},
            device_id_type=MESH,
        )

    def share(step, carry):
        shared(step).start()
        return carry

    def drain(u, carry):
        turned(u).wait_send()
        return carry

    def arrive(step, carry):
        shared(step).wait()
        return carry

    lax.fori_loop(1, n, share, 0)
    lax.fori_loop(1, m, drain, 0)
    lax.fori_loop(m + 1, n, drain, 0)
    lax.fori_loop(1, n, arrive, 0)

    everything = gathered[...]
    right = jnp.concatenate([everything[:, : half * SEARCH], everything[:, half * SEARCH :]], axis=0)
    bins = lax.broadcasted_iota(jnp.int32, (2 * trials, half * SEARCH), 1) % half
    out = jnp.zeros((2 * trials, half * SEARCH), f32)
    for k in range(half):
        out = jnp.where(bins == k, jnp.dot(twist[k], right, preferred_element_type=f32), out)
    out = out.T.reshape(SEARCH, half, 2 * trials)
    plane[:, :half, :] = out[:, :, :trials]
    plane[:, half:, :] = out[:, :, trials:]


def crate_device(n, voltages, gains, positions, directions, input_order, delays, search_beams):
    window, dft, spread = constant_tables()
    local = CH // n
    rows = 2 * local
    trials = TRIALS // n
    half = TIME // 2
    f32, bf16 = jnp.float32, jnp.bfloat16
    vmem = pl.BlockSpec(memory_space=pltpu.VMEM)
    power, plane = pl.pallas_call(
        functools.partial(crate_kernel, n),
        out_shape=(
            jax.ShapeDtypeStruct((local, TIME, BEAMS), f32),
            jax.ShapeDtypeStruct((SEARCH, TIME, trials), f32),
        ),
        in_specs=[vmem] * 10,
        out_specs=(vmem, vmem),
        scratch_shapes=[
            pltpu.VMEM((2 * CH, FFTLEN), bf16),
            pltpu.VMEM((TIME * 2 * CH, LANES), f32),
            pltpu.VMEM((n, rows, TIME, LANES), bf16),
            pltpu.VMEM((n, rows, TIME, LANES), bf16),
            pltpu.VMEM((48, INPUTS), bf16),
            pltpu.VMEM((LANES, LANES), f32),
            pltpu.VMEM((2, local, 2 * LANES, BEAMS), bf16),
            pltpu.VMEM((local, 2 * TIME, BEAMS), f32),
            pltpu.VMEM((half, 2 * trials, 2 * CH), bf16),
            pltpu.VMEM((BEAMS, TIME * SEARCH), bf16),
            pltpu.VMEM((local, TIME * SEARCH), bf16),
            pltpu.VMEM((CH, TIME * SEARCH), bf16),
            pltpu.VMEM((local, 2, INPUTS // 2), f32),
            pltpu.VMEM((local, 2 * TIME, BEAMS), bf16),
            pltpu.VMEM((local, 2 * TIME, BEAMS), bf16),
            pltpu.SemaphoreType.DMA((n,)),
            pltpu.SemaphoreType.DMA((n,)),
            pltpu.SemaphoreType.DMA((2,)),
            pltpu.SemaphoreType.DMA((n,)),
            pltpu.SemaphoreType.DMA((n,)),
            pltpu.SemaphoreType.DMA((2,)),
            pltpu.SemaphoreType.DMA((local,)),
            pltpu.SemaphoreType.DMA((local,)),
        ],
        compiler_params=pltpu.CompilerParams(
            collective_id=0, has_side_effects=True, vmem_limit_bytes=56 * 1024 * 1024
        ),
    )(
        voltages,
        jnp.asarray(window),
        jnp.asarray(dft),
        gains,
        positions,
        directions,
        input_order[None, :],
        delays,
        search_beams[None, :],
        jnp.asarray(spread),
    )
    return jnp.swapaxes(power, 1, 2), plane.transpose(2, 0, 1)


def solution(mesh):
    in_specs = (P(("groups", "crate"), None), P("crate", None, None), P(), P(), P(), P(), P())
    out_specs = (P(("groups", "crate"), None, None), P(("groups", "crate"), None, None))
    n = mesh.shape["crate"]
    fits = n % 2 == 0 and INPUTS // n == LANES and (CH // n) % 16 == 0 and (TRIALS // n) % 16 == 0
    body = functools.partial(crate_device, n) if fits else plain_device
    return jax.shard_map(body, mesh=mesh, in_specs=in_specs, out_specs=out_specs, check_vma=False)
```

```python
import functools
import math

import jax
import jax.numpy as jnp
import numpy as np
from jax import lax
from jax.experimental import pallas as pl
from jax.experimental.pallas import tpu as pltpu
from jax.sharding import PartitionSpec as P

INPUTS = 2048
CH = 256
BEAMS = 512
TRIALS = 1024
TAPS = 4
TIME = 32
SEARCH = 16
FFTLEN = 512


TWO_PI = 2.0 * math.pi


def pfb_window():
    window_len = TAPS * FFTLEN
    sample_index = jnp.arange(window_len, dtype=jnp.int32).astype(jnp.float32)
    offsets = (sample_index - 0.5 * window_len + 0.5) / FFTLEN
    tapering = 0.54 - 0.46 * jnp.cos(TWO_PI * sample_index / (window_len - 1))
    return (jnp.sinc(offsets) * tapering).reshape(TAPS, FFTLEN)


def fold_frames(voltages, window):
    frames = voltages.reshape(voltages.shape[0], TIME + TAPS - 1, FFTLEN)
    summed = window[0] * frames[:, 0:TIME].astype(jnp.float32)
    for tap_index in range(1, TAPS):
        summed = summed + window[tap_index] * frames[:, tap_index : tap_index + TIME].astype(
            jnp.float32
        )
    return summed.astype(jnp.bfloat16)


def dft_table():
    channel_ids = jnp.arange(CH, dtype=jnp.int32)[:, None]
    sample_ids = jnp.arange(FFTLEN, dtype=jnp.int32)[None, :]
    angles = TWO_PI * (channel_ids * sample_ids % FFTLEN).astype(jnp.float32) / FFTLEN
    factor = 1.0 / math.sqrt(FFTLEN)
    stacked = jnp.stack([jnp.cos(angles) * factor, -jnp.sin(angles) * factor], axis=1)
    return stacked.reshape(2 * CH, FFTLEN).astype(jnp.bfloat16)


def time_table():
    step_ids = jnp.arange(TIME, dtype=jnp.int32)[:, None]
    bin_ids = jnp.arange(1, TIME // 2 + 1, dtype=jnp.int32)[None, :]
    angles = TWO_PI * (step_ids * bin_ids % TIME).astype(jnp.float32) / TIME
    factor = 1.0 / math.sqrt(TIME)
    return jnp.concatenate([jnp.cos(angles) * factor, -jnp.sin(angles) * factor], axis=1)


def array_geometry(positions, directions, input_order):
    placed = jnp.take(positions, input_order, axis=1)
    geometry = directions[0][:, None] * placed[0][None, :]
    geometry = geometry + directions[1][:, None] * placed[1][None, :]
    return geometry + directions[2][:, None] * placed[2][None, :]


def steering(geometry, gain_row, frequency):
    phases = TWO_PI * frequency * geometry
    cosine = jnp.cos(phases)
    sine_part = jnp.sin(phases)
    weight_norm = 1.0 / math.sqrt(INPUTS)
    w_real = ((gain_row[0] * cosine + gain_row[1] * sine_part) * weight_norm).astype(jnp.bfloat16)
    w_imag = ((gain_row[1] * cosine - gain_row[0] * sine_part) * weight_norm).astype(jnp.bfloat16)
    upper_rows = jnp.concatenate([w_real, -w_imag], axis=1)
    lower_rows = jnp.concatenate([w_imag, w_real], axis=1)
    return jnp.concatenate([upper_rows, lower_rows], axis=0)


def dedisperse(spectrum, delay_part):
    half_bins = TIME // 2
    bin_ids = jnp.arange(1, half_bins + 1, dtype=jnp.int32)
    turn_counts = delay_part[:, :, None] * bin_ids[None, None, :] % TIME
    angles = TWO_PI * turn_counts.astype(jnp.float32) / TIME
    cosine = jnp.cos(angles)
    sine_part = jnp.sin(angles)
    spec_real = spectrum[:, :, :half_bins]
    spec_imag = spectrum[:, :, half_bins:]
    highest = lax.Precision.HIGHEST
    out_real = jnp.einsum(
        "cbk,dck->dbk", spec_real, cosine, precision=highest, preferred_element_type=jnp.float32
    ) - jnp.einsum(
        "cbk,dck->dbk", spec_imag, sine_part, precision=highest, preferred_element_type=jnp.float32
    )
    out_imag = jnp.einsum(
        "cbk,dck->dbk", spec_real, sine_part, precision=highest, preferred_element_type=jnp.float32
    ) + jnp.einsum(
        "cbk,dck->dbk", spec_imag, cosine, precision=highest, preferred_element_type=jnp.float32
    )
    factor = 1.0 / math.sqrt(CH)
    return jnp.concatenate([out_real, out_imag], axis=2) * factor


def plain_device(voltages, gains, positions, directions, input_order, delays, search_beams):
    window = pfb_window()
    folded = fold_frames(voltages, window)
    spectra = jnp.einsum("ks,its->kit", dft_table(), folded, preferred_element_type=jnp.float32)
    spectra = spectra.astype(jnp.bfloat16).reshape(CH, 2, voltages.shape[0], TIME)
    geometry = array_geometry(positions, directions, input_order)
    turned = lax.all_to_all(spectra, "crate", split_axis=0, concat_axis=2, tiled=True)
    local_count = turned.shape[0]
    first_channel = lax.axis_index("crate") * local_count

    def one_channel(packed):
        offsets, channel_data, gain_row = packed
        frequency = 1.0 + (first_channel + offsets).astype(jnp.float32) / CH
        weights = steering(geometry, gain_row, frequency)
        beam_sums = jnp.dot(
            weights,
            channel_data.reshape(2 * INPUTS, channel_data.shape[-1]),
            preferred_element_type=jnp.float32,
        )
        return beam_sums[:BEAMS] * beam_sums[:BEAMS] + beam_sums[BEAMS:] * beam_sums[BEAMS:]

    beam_power = lax.map(one_channel, (jnp.arange(local_count, dtype=jnp.int32), turned, gains))
    local_channels = beam_power.shape[0]
    chosen = jnp.take(beam_power, search_beams, axis=1)
    power_spectra = jnp.dot(
        chosen.reshape(local_channels * SEARCH, TIME),
        time_table(),
        precision=lax.Precision.HIGHEST,
        preferred_element_type=jnp.float32,
    )
    power_spectra = power_spectra.reshape(local_channels, SEARCH, TIME)
    trial_rows = TRIALS // lax.axis_size("crate")
    first_trial = lax.axis_index("crate") * trial_rows
    own_delays = lax.dynamic_slice_in_dim(delays, first_trial, trial_rows, 0)
    dm_plane = dedisperse(lax.all_gather(power_spectra, "crate", axis=0, tiled=True), own_delays)
    return (beam_power, dm_plane)


LANES = 128
MESH = pl.DeviceIdType.MESH


def constant_tables():
    n = np.arange(TAPS * FFTLEN, dtype=np.float64)
    u = (n - 0.5 * TAPS * FFTLEN + 0.5) / FFTLEN
    taper = 0.54 - 0.46 * np.cos(TWO_PI * n / (TAPS * FFTLEN - 1))
    window = (np.sinc(u) * taper).reshape(TAPS, FFTLEN).astype(np.float32)
    c = np.arange(CH)[:, None]
    s = np.arange(FFTLEN)[None, :]
    angles = TWO_PI * (c * s % FFTLEN) / FFTLEN
    table = np.stack([np.cos(angles), -np.sin(angles)], axis=1) / math.sqrt(FFTLEN)
    dft = table.reshape(2 * CH, FFTLEN).astype(np.float32)
    t = np.arange(TIME)[:, None]
    k = np.arange(1, TIME // 2 + 1)[None, :]
    turns = TWO_PI * (t * k % TIME) / TIME
    steps = np.concatenate([np.cos(turns), -np.sin(turns)], axis=1) / math.sqrt(TIME * CH)
    spread = np.concatenate(
        [np.tile(steps[:, : TIME // 2], (1, SEARCH)), np.tile(steps[:, TIME // 2 :], (1, SEARCH))],
        axis=1,
    ).astype(np.float32)
    return window, dft, spread


def series(function, degree):
    nodes = 0.125 + 0.125 * np.cos((2 * np.arange(400) + 1) * np.pi / 800)
    fit = np.polynomial.chebyshev.Chebyshev.fit(nodes, function(nodes), degree, domain=[0, 0.25])
    return [float(value) for value in fit.convert(kind=np.polynomial.Polynomial).coef[::-1]]


SINE = series(lambda z: np.pi * np.sinc(np.sqrt(z)), 4)
COSINE = series(lambda z: np.cos(np.pi * np.sqrt(z)), 4)
ROUNDER = 1.5 * 2.0**23


def turn(x):
    y = x - ((x + ROUNDER) - ROUNDER)
    z = y * y
    sine, cosine = SINE[0], COSINE[0]
    for value in SINE[1:]:
        sine = sine * z + value
    for value in COSINE[1:]:
        cosine = cosine * z + value
    sine = sine * y
    double = sine + sine
    return 1.0 - double * sine, double * cosine


def split_three(x):
    high = x.astype(jnp.bfloat16)
    left = x - high.astype(jnp.float32)
    middle = left.astype(jnp.bfloat16)
    return high, middle, (left - middle.astype(jnp.float32)).astype(jnp.bfloat16)


def crate_kernel(
    n, volts, window, dft, gains, positions, directions, order, delays, beams, spread,
    power, plane,
    table, folded, frames, sent, held, parts, columns, wheel, sums, twist, onehot, mine, gathered,
    lent, leaving, landing,
    send_sem, recv_sem, own_sem, share_send, share_recv, lend_sem, part_send, part_recv,
):
    me = lax.axis_index("crate")
    rows = 2 * CH // n
    local = CH // n
    trials = TRIALS // n
    half = TIME // 2
    f32, bf16 = jnp.float32, jnp.bfloat16

    m = n // 2
    side = me // m
    place_in = lax.rem(me, m)
    twin = (1 - side) * m + place_in

    def peer(step):
        return lax.rem(me + step, n)

    def near(u):
        return side * m + lax.rem(place_in + u, m)

    def owner(u):
        return side * m + lax.rem(place_in - u + 2 * m, m)

    def channel_side(u):
        return side + (1 - u // m) * (1 - 2 * side)

    barrier = pltpu.get_barrier_semaphore()

    def greet(step, carry):
        pl.semaphore_signal(barrier, inc=1, device_id={"crate": peer(step)}, device_id_type=MESH)
        return carry

    lax.fori_loop(1, n, greet, 0)

    table[...] = dft[...].astype(bf16)
    side_rows = m * rows

    def fold(t):
        total = None
        for tap in range(TAPS):
            at = pl.multiple_of((t + tap) * FFTLEN, FFTLEN)
            term = window[tap : tap + 1, :] * volts[:, pl.ds(at, FFTLEN)].astype(f32)
            total = term if total is None else total + term
        return total.astype(bf16)

    def channelize(which_side, first_time):
        begin = pl.multiple_of(which_side * side_rows, side_rows)

        def body(pair, carry):
            if first_time:
                folded[pair, :LANES] = fold(2 * pair)
                folded[pair, LANES:] = fold(2 * pair + 1)
            out = lax.dot_general(
                table[pl.ds(begin, side_rows), :],
                folded[pair],
                (((1,), (1,)), ((), ())),
                preferred_element_type=f32,
            )
            for which in range(2):
                at = pl.multiple_of((2 * pair + which) * 2 * CH + begin, side_rows)
                frames[pl.ds(at, side_rows), :] = out[:, which * LANES : (which + 1) * LANES]
            return carry

        lax.fori_loop(0, TIME // 2, body, 0, unroll=2)

    def pack(u):
        first = (channel_side(u) * m + lax.rem(place_in + u, m)) * rows
        for row in range(rows):
            sent[u, row] = frames[pl.ds(first + row, TIME, stride=2 * CH), :].astype(bf16)

    def turned(u):
        return pltpu.make_async_remote_copy(
            src_ref=sent.at[u],
            dst_ref=held.at[u],
            send_sem=send_sem.at[u],
            recv_sem=recv_sem.at[u],
            device_id={"crate": near(u)},
            device_id_type=MESH,
        )

    def partial(c):
        return pltpu.make_async_remote_copy(
            src_ref=leaving.at[c],
            dst_ref=landing.at[c],
            send_sem=part_send.at[c],
            recv_sem=part_recv.at[c],
            device_id={"crate": twin},
            device_id_type=MESH,
        )

    far = pl.ds(pl.multiple_of((1 - side) * (m * LANES), LANES), m * LANES)
    lend = pltpu.make_async_remote_copy(
        src_ref=gains.at[:, :, far],
        dst_ref=lent,
        send_sem=lend_sem.at[0],
        recv_sem=lend_sem.at[1],
        device_id={"crate": twin},
        device_id_type=MESH,
    )
    channelize(1 - side, True)
    pl.semaphore_wait(barrier, n - 1)
    lend.start()

    def send(u, carry):
        pack(u)
        turned(u).start()
        return carry

    lax.fori_loop(1, m, send, 0)
    pack(0)
    own_first = pltpu.make_async_copy(sent.at[0], held.at[0], own_sem.at[0])
    own_first.start()
    channelize(side, False)
    lax.fori_loop(m + 1, n, send, 0)
    pack(m)
    own_later = pltpu.make_async_copy(sent.at[m], held.at[m], own_sem.at[1])
    own_later.start()

    parts[...] = jnp.zeros_like(parts)
    for index, part in enumerate(split_three(positions[...])):
        parts[16 * index : 16 * index + 3] = part
    beam_ids = lax.broadcasted_iota(jnp.int32, (BEAMS, SEARCH), 0)
    listed = jnp.where(beam_ids == beams[...], 1.0, 0.0).astype(bf16)
    search_ids = lax.broadcasted_iota(jnp.int32, (SEARCH, TIME * SEARCH), 0)
    lane_ids = lax.broadcasted_iota(jnp.int32, (SEARCH, TIME * SEARCH), 1)
    widen = jnp.where(lane_ids // half % SEARCH == search_ids, 1.0, 0.0).astype(bf16)
    onehot[...] = jnp.dot(listed, widen, preferred_element_type=f32).astype(bf16)

    at = pl.multiple_of(me * trials, trials)
    cos_one, sin_one = turn(delays[pl.ds(at, trials), :].astype(f32) * (1.0 / TIME))
    cosine, sine = cos_one, sin_one
    for k in range(half):
        low = cosine.astype(bf16)
        high = sine.astype(bf16)
        twist[k, :trials, :CH] = low
        twist[k, :trials, CH:] = -high
        twist[k, trials:, :CH] = high
        twist[k, trials:, CH:] = low
        cosine, sine = cosine * cos_one - sine * sin_one, sine * cos_one + cosine * sin_one

    sums[...] = jnp.zeros_like(sums)
    own_first.wait()
    own_later.wait()

    def place(u):
        at = pl.multiple_of(owner(u) * LANES, LANES)
        antenna = lax.broadcasted_iota(jnp.int32, (INPUTS, LANES), 0)
        pick = jnp.where(antenna == order[:, pl.ds(at, LANES)], 1.0, 0.0).astype(bf16)
        out = jnp.dot(parts[...], pick, preferred_element_type=f32)
        placed = out[0:16] + out[16:32] + out[32:48]
        columns[lax.rem(u, m)] = jnp.concatenate([placed] * (LANES // 16), axis=0).T

    def steer(block, slot, u):
        first_channel = (channel_side(u) * m + place_in) * local
        start = 1.0 + first_channel.astype(f32) * (1.0 / CH)
        first = pl.multiple_of(block * 16, 16)
        p = columns[lax.rem(u, m), pl.ds(first, 16), :]
        width = BEAMS // 2
        for side in range(2):
            lanes = slice(side * width, (side + 1) * width)
            turns = p[:, 0:1] * directions[0:1, lanes]
            turns = turns + p[:, 1:2] * directions[1:2, lanes]
            turns = turns + p[:, 2:3] * directions[2:3, lanes]
            cosine, sine = turn(turns * start)
            cos_step, sin_step = turn(turns * (1.0 / CH))
            real, imag = cosine, -sine
            ahead = (real * cos_step + imag * sin_step, imag * cos_step - real * sin_step)
            twice = 2.0 * cos_step
            for c in range(local):
                wheel[slot, c, pl.ds(first, 16), lanes] = real.astype(bf16)
                wheel[slot, c, pl.ds(LANES + first, 16), lanes] = imag.astype(bf16)
                if c + 1 < local:
                    after = (twice * ahead[0] - real, twice * ahead[1] - imag)
                    (real, imag), ahead = ahead, after

    def add_channel(c, step, slot, gain_ref, at):
        gain = gain_ref[c, :, pl.ds(at, LANES)] * (1.0 / math.sqrt(INPUTS))
        gain_real, gain_imag = gain[0:1], gain[1:2]
        real = held[step, 2 * c].astype(f32)
        imag = held[step, 2 * c + 1].astype(f32)
        y_real = (gain_real * real - gain_imag * imag).astype(bf16)
        y_imag = (gain_real * imag + gain_imag * real).astype(bf16)
        left = jnp.concatenate(
            [
                jnp.concatenate([y_real, -y_imag], axis=1),
                jnp.concatenate([y_imag, y_real], axis=1),
            ],
            axis=0,
        )
        sums[c] += jnp.dot(left, wheel[slot, c], preferred_element_type=f32)

    blocks = LANES // 16
    per_block = local // blocks

    def add_source(u, later, steering_on, finish=None):
        slot = lax.rem(u, 2)
        gain_ref = gains if later else lent
        source = owner(u) if later else owner(u) - side * m
        at = pl.multiple_of(source * LANES, LANES)

        def body(block, carry):
            if steering_on:
                steer(block, 1 - slot, u + 1)
            for c in range(per_block):
                add_channel(block * per_block + c, u, slot, gain_ref, at)
                if finish is not None:
                    finish(block * per_block + c)
            return carry

        lax.fori_loop(0, blocks, body, 0, unroll=1 if steering_on else 4)

    def first_steer(block, carry):
        steer(block, 0, 0)
        return carry

    def place_all(u, carry):
        place(u)
        return carry

    place(0)
    lax.fori_loop(0, blocks, first_steer, 0)
    lax.fori_loop(1, m, place_all, 0)
    lend.wait()
    add_source(0, False, True)

    def for_twin(u, carry):
        turned(u).wait_recv()
        add_source(u, False, True)
        return carry

    def hand_over(c):
        leaving[c] = sums[c].astype(bf16)
        partial(c).start()
        sums[c] = jnp.zeros((2 * TIME, BEAMS), f32)

    lax.fori_loop(1, m - 1, for_twin, 0)
    turned(m - 1).wait_recv()
    add_source(m - 1, False, True, hand_over)
    add_source(m, True, True)

    def for_self(u, carry):
        turned(u).wait_recv()
        add_source(u, True, True)
        return carry

    lax.fori_loop(m + 1, n - 1, for_self, 0)
    turned(n - 1).wait_recv()

    def detect(c):
        partial(c).wait()
        total = sums[c] + landing[c].astype(f32)
        power[c] = total[:TIME] * total[:TIME] + total[TIME:] * total[TIME:]

    add_source(n - 1, True, False, detect)
    flat = power[...].reshape(local * TIME, BEAMS)
    high = flat.astype(bf16)
    low = (flat - high.astype(f32)).astype(bf16)
    chosen = jnp.dot(high, onehot[...], preferred_element_type=f32) + jnp.dot(
        low, onehot[...], preferred_element_type=f32
    )
    chosen = chosen.reshape(local, TIME, TIME * SEARCH) * spread[...][None]
    mine[...] = jnp.sum(chosen, axis=1).astype(bf16)
    here = pl.ds(pl.multiple_of(me * local, local), local)
    gathered[here, :] = mine[...]

    def shared(step):
        return pltpu.make_async_remote_copy(
            src_ref=mine,
            dst_ref=gathered.at[here],
            send_sem=share_send.at[step],
            recv_sem=share_recv.at[step],
            device_id={"crate": peer(step)},
            device_id_type=MESH,
        )

    def share(step, carry):
        shared(step).start()
        return carry

    def drain(u, carry):
        turned(u).wait_send()
        return carry

    def arrive(step, carry):
        shared(step).wait()
        return carry

    lax.fori_loop(1, n, share, 0)
    lax.fori_loop(1, m, drain, 0)
    lax.fori_loop(m + 1, n, drain, 0)
    lax.fori_loop(1, n, arrive, 0)

    everything = gathered[...]
    right = jnp.concatenate([everything[:, : half * SEARCH], everything[:, half * SEARCH :]], axis=0)
    bins = lax.broadcasted_iota(jnp.int32, (2 * trials, half * SEARCH), 1) % half
    out = jnp.zeros((2 * trials, half * SEARCH), f32)
    for k in range(half):
        out = jnp.where(bins == k, jnp.dot(twist[k], right, preferred_element_type=f32), out)
    out = out.T.reshape(SEARCH, half, 2 * trials)
    plane[:, :half, :] = out[:, :, :trials]
    plane[:, half:, :] = out[:, :, trials:]


def crate_device(n, voltages, gains, positions, directions, input_order, delays, search_beams):
    window, dft, spread = constant_tables()
    local = CH // n
    rows = 2 * local
    trials = TRIALS // n
    half = TIME // 2
    f32, bf16 = jnp.float32, jnp.bfloat16
    vmem = pl.BlockSpec(memory_space=pltpu.VMEM)
    power, plane = pl.pallas_call(
        functools.partial(crate_kernel, n),
        out_shape=(
            jax.ShapeDtypeStruct((local, TIME, BEAMS), f32),
            jax.ShapeDtypeStruct((SEARCH, TIME, trials), f32),
        ),
        in_specs=[vmem] * 10,
        out_specs=(vmem, vmem),
        scratch_shapes=[
            pltpu.VMEM((2 * CH, FFTLEN), bf16),
            pltpu.VMEM((TIME // 2, 2 * LANES, FFTLEN), bf16),
            pltpu.VMEM((TIME * 2 * CH, LANES), f32),
            pltpu.VMEM((n, rows, TIME, LANES), bf16),
            pltpu.VMEM((n, rows, TIME, LANES), bf16),
            pltpu.VMEM((48, INPUTS), bf16),
            pltpu.VMEM((n // 2, LANES, LANES), f32),
            pltpu.VMEM((2, local, 2 * LANES, BEAMS), bf16),
            pltpu.VMEM((local, 2 * TIME, BEAMS), f32),
            pltpu.VMEM((half, 2 * trials, 2 * CH), bf16),
            pltpu.VMEM((BEAMS, TIME * SEARCH), bf16),
            pltpu.VMEM((local, TIME * SEARCH), bf16),
            pltpu.VMEM((CH, TIME * SEARCH), bf16),
            pltpu.VMEM((local, 2, INPUTS // 2), f32),
            pltpu.VMEM((local, 2 * TIME, BEAMS), bf16),
            pltpu.VMEM((local, 2 * TIME, BEAMS), bf16),
            pltpu.SemaphoreType.DMA((n,)),
            pltpu.SemaphoreType.DMA((n,)),
            pltpu.SemaphoreType.DMA((2,)),
            pltpu.SemaphoreType.DMA((n,)),
            pltpu.SemaphoreType.DMA((n,)),
            pltpu.SemaphoreType.DMA((2,)),
            pltpu.SemaphoreType.DMA((local,)),
            pltpu.SemaphoreType.DMA((local,)),
        ],
        compiler_params=pltpu.CompilerParams(
            collective_id=0, has_side_effects=True, vmem_limit_bytes=56 * 1024 * 1024
        ),
    )(
        voltages,
        jnp.asarray(window),
        jnp.asarray(dft),
        gains,
        positions,
        directions,
        input_order[None, :],
        delays,
        search_beams[None, :],
        jnp.asarray(spread),
    )
    return jnp.swapaxes(power, 1, 2), plane.transpose(2, 0, 1)


def solution(mesh):
    in_specs = (P(("groups", "crate"), None), P("crate", None, None), P(), P(), P(), P(), P())
    out_specs = (P(("groups", "crate"), None, None), P(("groups", "crate"), None, None))
    n = mesh.shape["crate"]
    fits = n % 2 == 0 and INPUTS // n == LANES and (CH // n) % 16 == 0 and (TRIALS // n) % 16 == 0
    body = functools.partial(crate_device, n) if fits else plain_device
    return jax.shard_map(body, mesh=mesh, in_specs=in_specs, out_specs=out_specs, check_vma=False)
```

```python
import functools
import math

import jax
import jax.numpy as jnp
import numpy as np
from jax import lax
from jax.experimental import pallas as pl
from jax.experimental.pallas import tpu as pltpu
from jax.sharding import PartitionSpec as P

INPUTS = 2048
CH = 256
BEAMS = 512
TRIALS = 1024
TAPS = 4
TIME = 32
SEARCH = 16
FFTLEN = 512


TWO_PI = 2.0 * math.pi


def pfb_window():
    window_len = TAPS * FFTLEN
    sample_index = jnp.arange(window_len, dtype=jnp.int32).astype(jnp.float32)
    offsets = (sample_index - 0.5 * window_len + 0.5) / FFTLEN
    tapering = 0.54 - 0.46 * jnp.cos(TWO_PI * sample_index / (window_len - 1))
    return (jnp.sinc(offsets) * tapering).reshape(TAPS, FFTLEN)


def fold_frames(voltages, window):
    frames = voltages.reshape(voltages.shape[0], TIME + TAPS - 1, FFTLEN)
    summed = window[0] * frames[:, 0:TIME].astype(jnp.float32)
    for tap_index in range(1, TAPS):
        summed = summed + window[tap_index] * frames[:, tap_index : tap_index + TIME].astype(
            jnp.float32
        )
    return summed.astype(jnp.bfloat16)


def dft_table():
    channel_ids = jnp.arange(CH, dtype=jnp.int32)[:, None]
    sample_ids = jnp.arange(FFTLEN, dtype=jnp.int32)[None, :]
    angles = TWO_PI * (channel_ids * sample_ids % FFTLEN).astype(jnp.float32) / FFTLEN
    factor = 1.0 / math.sqrt(FFTLEN)
    stacked = jnp.stack([jnp.cos(angles) * factor, -jnp.sin(angles) * factor], axis=1)
    return stacked.reshape(2 * CH, FFTLEN).astype(jnp.bfloat16)


def time_table():
    step_ids = jnp.arange(TIME, dtype=jnp.int32)[:, None]
    bin_ids = jnp.arange(1, TIME // 2 + 1, dtype=jnp.int32)[None, :]
    angles = TWO_PI * (step_ids * bin_ids % TIME).astype(jnp.float32) / TIME
    factor = 1.0 / math.sqrt(TIME)
    return jnp.concatenate([jnp.cos(angles) * factor, -jnp.sin(angles) * factor], axis=1)


def array_geometry(positions, directions, input_order):
    placed = jnp.take(positions, input_order, axis=1)
    geometry = directions[0][:, None] * placed[0][None, :]
    geometry = geometry + directions[1][:, None] * placed[1][None, :]
    return geometry + directions[2][:, None] * placed[2][None, :]


def steering(geometry, gain_row, frequency):
    phases = TWO_PI * frequency * geometry
    cosine = jnp.cos(phases)
    sine_part = jnp.sin(phases)
    weight_norm = 1.0 / math.sqrt(INPUTS)
    w_real = ((gain_row[0] * cosine + gain_row[1] * sine_part) * weight_norm).astype(jnp.bfloat16)
    w_imag = ((gain_row[1] * cosine - gain_row[0] * sine_part) * weight_norm).astype(jnp.bfloat16)
    upper_rows = jnp.concatenate([w_real, -w_imag], axis=1)
    lower_rows = jnp.concatenate([w_imag, w_real], axis=1)
    return jnp.concatenate([upper_rows, lower_rows], axis=0)


def dedisperse(spectrum, delay_part):
    half_bins = TIME // 2
    bin_ids = jnp.arange(1, half_bins + 1, dtype=jnp.int32)
    turn_counts = delay_part[:, :, None] * bin_ids[None, None, :] % TIME
    angles = TWO_PI * turn_counts.astype(jnp.float32) / TIME
    cosine = jnp.cos(angles)
    sine_part = jnp.sin(angles)
    spec_real = spectrum[:, :, :half_bins]
    spec_imag = spectrum[:, :, half_bins:]
    highest = lax.Precision.HIGHEST
    out_real = jnp.einsum(
        "cbk,dck->dbk", spec_real, cosine, precision=highest, preferred_element_type=jnp.float32
    ) - jnp.einsum(
        "cbk,dck->dbk", spec_imag, sine_part, precision=highest, preferred_element_type=jnp.float32
    )
    out_imag = jnp.einsum(
        "cbk,dck->dbk", spec_real, sine_part, precision=highest, preferred_element_type=jnp.float32
    ) + jnp.einsum(
        "cbk,dck->dbk", spec_imag, cosine, precision=highest, preferred_element_type=jnp.float32
    )
    factor = 1.0 / math.sqrt(CH)
    return jnp.concatenate([out_real, out_imag], axis=2) * factor


def plain_device(voltages, gains, positions, directions, input_order, delays, search_beams):
    window = pfb_window()
    folded = fold_frames(voltages, window)
    spectra = jnp.einsum("ks,its->kit", dft_table(), folded, preferred_element_type=jnp.float32)
    spectra = spectra.astype(jnp.bfloat16).reshape(CH, 2, voltages.shape[0], TIME)
    geometry = array_geometry(positions, directions, input_order)
    turned = lax.all_to_all(spectra, "crate", split_axis=0, concat_axis=2, tiled=True)
    local_count = turned.shape[0]
    first_channel = lax.axis_index("crate") * local_count

    def one_channel(packed):
        offsets, channel_data, gain_row = packed
        frequency = 1.0 + (first_channel + offsets).astype(jnp.float32) / CH
        weights = steering(geometry, gain_row, frequency)
        beam_sums = jnp.dot(
            weights,
            channel_data.reshape(2 * INPUTS, channel_data.shape[-1]),
            preferred_element_type=jnp.float32,
        )
        return beam_sums[:BEAMS] * beam_sums[:BEAMS] + beam_sums[BEAMS:] * beam_sums[BEAMS:]

    beam_power = lax.map(one_channel, (jnp.arange(local_count, dtype=jnp.int32), turned, gains))
    local_channels = beam_power.shape[0]
    chosen = jnp.take(beam_power, search_beams, axis=1)
    power_spectra = jnp.dot(
        chosen.reshape(local_channels * SEARCH, TIME),
        time_table(),
        precision=lax.Precision.HIGHEST,
        preferred_element_type=jnp.float32,
    )
    power_spectra = power_spectra.reshape(local_channels, SEARCH, TIME)
    trial_rows = TRIALS // lax.axis_size("crate")
    first_trial = lax.axis_index("crate") * trial_rows
    own_delays = lax.dynamic_slice_in_dim(delays, first_trial, trial_rows, 0)
    dm_plane = dedisperse(lax.all_gather(power_spectra, "crate", axis=0, tiled=True), own_delays)
    return (beam_power, dm_plane)


LANES = 128
MESH = pl.DeviceIdType.MESH


def constant_tables():
    n = np.arange(TAPS * FFTLEN, dtype=np.float64)
    u = (n - 0.5 * TAPS * FFTLEN + 0.5) / FFTLEN
    taper = 0.54 - 0.46 * np.cos(TWO_PI * n / (TAPS * FFTLEN - 1))
    window = (np.sinc(u) * taper).reshape(TAPS, FFTLEN).astype(np.float32)
    c = np.arange(CH)[:, None]
    s = np.arange(FFTLEN)[None, :]
    angles = TWO_PI * (c * s % FFTLEN) / FFTLEN
    table = np.stack([np.cos(angles), -np.sin(angles)], axis=1) / math.sqrt(FFTLEN)
    dft = table.reshape(2 * CH, FFTLEN).astype(np.float32)
    t = np.arange(TIME)[:, None]
    k = np.arange(1, TIME // 2 + 1)[None, :]
    turns = TWO_PI * (t * k % TIME) / TIME
    steps = np.concatenate([np.cos(turns), -np.sin(turns)], axis=1) / math.sqrt(TIME * CH)
    spread = np.concatenate(
        [np.tile(steps[:, : TIME // 2], (1, SEARCH)), np.tile(steps[:, TIME // 2 :], (1, SEARCH))],
        axis=1,
    ).astype(np.float32)
    return window, dft, spread


def series(function, degree):
    nodes = 0.125 + 0.125 * np.cos((2 * np.arange(400) + 1) * np.pi / 800)
    fit = np.polynomial.chebyshev.Chebyshev.fit(nodes, function(nodes), degree, domain=[0, 0.25])
    return [float(value) for value in fit.convert(kind=np.polynomial.Polynomial).coef[::-1]]


SINE = series(lambda z: np.pi * np.sinc(np.sqrt(z)), 4)
COSINE = series(lambda z: np.cos(np.pi * np.sqrt(z)), 4)
ROUNDER = 1.5 * 2.0**23


def turn(x):
    y = x - ((x + ROUNDER) - ROUNDER)
    z = y * y
    sine, cosine = SINE[0], COSINE[0]
    for value in SINE[1:]:
        sine = sine * z + value
    for value in COSINE[1:]:
        cosine = cosine * z + value
    sine = sine * y
    double = sine + sine
    return 1.0 - double * sine, double * cosine


def split_three(x):
    high = x.astype(jnp.bfloat16)
    left = x - high.astype(jnp.float32)
    middle = left.astype(jnp.bfloat16)
    return high, middle, (left - middle.astype(jnp.float32)).astype(jnp.bfloat16)


def crate_kernel(
    n, volts, window, dft, gains, positions, directions, order, delays, beams, spread,
    power, plane,
    table, folded, frames, sent, held, parts, columns, wheel, sums, twist, onehot, mine, gathered,
    lent, leaving, landing,
    send_sem, recv_sem, own_sem, share_send, share_recv, lend_sem, part_send, part_recv,
):
    me = lax.axis_index("crate")
    rows = 2 * CH // n
    local = CH // n
    trials = TRIALS // n
    half = TIME // 2
    f32, bf16 = jnp.float32, jnp.bfloat16

    m = n // 2
    side = me // m
    place_in = lax.rem(me, m)
    twin = (1 - side) * m + place_in

    def peer(step):
        return lax.rem(me + step, n)

    w = m // 2
    layer = place_in // w
    seat = lax.rem(place_in, w)

    def layer_of(u):
        return lax.rem(layer + u % m // w, 2) * w

    def spot(u):
        return layer_of(u) + lax.rem(seat + u, w)

    def near(u):
        return side * m + spot(u)

    def owner(u):
        return side * m + layer_of(u) + lax.rem(seat - u + 2 * m, w)

    def channel_side(u):
        return side + (1 - u // m) * (1 - 2 * side)

    barrier = pltpu.get_barrier_semaphore()

    def greet(step, carry):
        pl.semaphore_signal(barrier, inc=1, device_id={"crate": peer(step)}, device_id_type=MESH)
        return carry

    lax.fori_loop(1, n, greet, 0)

    table[...] = dft[...].astype(bf16)
    side_rows = m * rows

    def fold(t):
        total = None
        for tap in range(TAPS):
            at = pl.multiple_of((t + tap) * FFTLEN, FFTLEN)
            term = window[tap : tap + 1, :] * volts[:, pl.ds(at, FFTLEN)].astype(f32)
            total = term if total is None else total + term
        return total.astype(bf16)

    def channelize(which_side, first_time):
        begin = pl.multiple_of(which_side * side_rows, side_rows)

        def body(pair, carry):
            if first_time:
                folded[pair, :LANES] = fold(2 * pair)
                folded[pair, LANES:] = fold(2 * pair + 1)
            out = lax.dot_general(
                table[pl.ds(begin, side_rows), :],
                folded[pair],
                (((1,), (1,)), ((), ())),
                preferred_element_type=f32,
            )
            for which in range(2):
                at = pl.multiple_of((2 * pair + which) * 2 * CH + begin, side_rows)
                frames[pl.ds(at, side_rows), :] = out[:, which * LANES : (which + 1) * LANES]
            return carry

        lax.fori_loop(0, TIME // 2, body, 0, unroll=2)

    def pack(u):
        first = (channel_side(u) * m + spot(u)) * rows
        for row in range(rows):
            sent[u, row] = frames[pl.ds(first + row, TIME, stride=2 * CH), :].astype(bf16)

    def turned(u):
        return pltpu.make_async_remote_copy(
            src_ref=sent.at[u],
            dst_ref=held.at[u],
            send_sem=send_sem.at[u],
            recv_sem=recv_sem.at[u],
            device_id={"crate": near(u)},
            device_id_type=MESH,
        )

    def partial(c):
        return pltpu.make_async_remote_copy(
            src_ref=leaving.at[c],
            dst_ref=landing.at[c],
            send_sem=part_send.at[c],
            recv_sem=part_recv.at[c],
            device_id={"crate": twin},
            device_id_type=MESH,
        )

    far = pl.ds(pl.multiple_of((1 - side) * (m * LANES), LANES), m * LANES)
    lend = pltpu.make_async_remote_copy(
        src_ref=gains.at[:, :, far],
        dst_ref=lent,
        send_sem=lend_sem.at[0],
        recv_sem=lend_sem.at[1],
        device_id={"crate": twin},
        device_id_type=MESH,
    )
    channelize(1 - side, True)
    pl.semaphore_wait(barrier, n - 1)
    lend.start()

    def send(u, carry):
        pack(u)
        turned(u).start()
        return carry

    lax.fori_loop(w, m, send, 0)
    lax.fori_loop(1, w, send, 0)
    pack(0)
    own_first = pltpu.make_async_copy(sent.at[0], held.at[0], own_sem.at[0])
    own_first.start()
    channelize(side, False)

    def prepare(u, carry):
        pack(u)
        return carry

    lax.fori_loop(m, n, prepare, 0)
    own_later = pltpu.make_async_copy(sent.at[m], held.at[m], own_sem.at[1])
    own_later.start()

    parts[...] = jnp.zeros_like(parts)
    for index, part in enumerate(split_three(positions[...])):
        parts[16 * index : 16 * index + 3] = part
    beam_ids = lax.broadcasted_iota(jnp.int32, (BEAMS, SEARCH), 0)
    listed = jnp.where(beam_ids == beams[...], 1.0, 0.0).astype(bf16)
    search_ids = lax.broadcasted_iota(jnp.int32, (SEARCH, TIME * SEARCH), 0)
    lane_ids = lax.broadcasted_iota(jnp.int32, (SEARCH, TIME * SEARCH), 1)
    widen = jnp.where(lane_ids // half % SEARCH == search_ids, 1.0, 0.0).astype(bf16)
    onehot[...] = jnp.dot(listed, widen, preferred_element_type=f32).astype(bf16)

    at = pl.multiple_of(me * trials, trials)
    cos_one, sin_one = turn(delays[pl.ds(at, trials), :].astype(f32) * (1.0 / TIME))
    cosine, sine = cos_one, sin_one
    for k in range(half):
        low = cosine.astype(bf16)
        high = sine.astype(bf16)
        twist[k, :trials, :CH] = low
        twist[k, :trials, CH:] = -high
        twist[k, trials:, :CH] = high
        twist[k, trials:, CH:] = low
        cosine, sine = cosine * cos_one - sine * sin_one, sine * cos_one + cosine * sin_one

    sums[...] = jnp.zeros_like(sums)
    own_first.wait()
    own_later.wait()

    def place(u):
        at = pl.multiple_of(owner(u) * LANES, LANES)
        antenna = lax.broadcasted_iota(jnp.int32, (INPUTS, LANES), 0)
        pick = jnp.where(antenna == order[:, pl.ds(at, LANES)], 1.0, 0.0).astype(bf16)
        out = jnp.dot(parts[...], pick, preferred_element_type=f32)
        placed = out[0:16] + out[16:32] + out[32:48]
        columns[lax.rem(u, m)] = jnp.concatenate([placed] * (LANES // 16), axis=0).T

    def steer(block, slot, u):
        first_channel = (channel_side(u) * m + place_in) * local
        start = 1.0 + first_channel.astype(f32) * (1.0 / CH)
        first = pl.multiple_of(block * 16, 16)
        p = columns[lax.rem(u, m), pl.ds(first, 16), :]
        width = BEAMS // 2
        for side in range(2):
            lanes = slice(side * width, (side + 1) * width)
            turns = p[:, 0:1] * directions[0:1, lanes]
            turns = turns + p[:, 1:2] * directions[1:2, lanes]
            turns = turns + p[:, 2:3] * directions[2:3, lanes]
            cosine, sine = turn(turns * start)
            cos_step, sin_step = turn(turns * (1.0 / CH))
            real, imag = cosine, -sine
            ahead = (real * cos_step + imag * sin_step, imag * cos_step - real * sin_step)
            twice = 2.0 * cos_step
            for c in range(local):
                wheel[slot, c, pl.ds(first, 16), lanes] = real.astype(bf16)
                wheel[slot, c, pl.ds(LANES + first, 16), lanes] = imag.astype(bf16)
                if c + 1 < local:
                    after = (twice * ahead[0] - real, twice * ahead[1] - imag)
                    (real, imag), ahead = ahead, after

    def add_channel(c, step, slot, gain_ref, at):
        gain = gain_ref[c, :, pl.ds(at, LANES)] * (1.0 / math.sqrt(INPUTS))
        gain_real, gain_imag = gain[0:1], gain[1:2]
        real = held[step, 2 * c].astype(f32)
        imag = held[step, 2 * c + 1].astype(f32)
        y_real = (gain_real * real - gain_imag * imag).astype(bf16)
        y_imag = (gain_real * imag + gain_imag * real).astype(bf16)
        left = jnp.concatenate(
            [
                jnp.concatenate([y_real, -y_imag], axis=1),
                jnp.concatenate([y_imag, y_real], axis=1),
            ],
            axis=0,
        )
        sums[c] += jnp.dot(left, wheel[slot, c], preferred_element_type=f32)

    blocks = LANES // 16
    per_block = local // blocks

    def add_source(u, later, steering_on, finish=None):
        slot = lax.rem(u, 2)
        gain_ref = gains if later else lent
        source = owner(u) if later else owner(u) - side * m
        at = pl.multiple_of(source * LANES, LANES)

        def body(block, carry):
            if steering_on:
                steer(block, 1 - slot, u + 1)
            for c in range(per_block):
                add_channel(block * per_block + c, u, slot, gain_ref, at)
                if finish is not None:
                    finish(block * per_block + c)
            return carry

        lax.fori_loop(0, blocks, body, 0, unroll=1 if steering_on else 4)

    def first_steer(block, carry):
        steer(block, 0, 0)
        return carry

    def place_all(u, carry):
        place(u)
        return carry

    place(0)
    lax.fori_loop(0, blocks, first_steer, 0)
    lax.fori_loop(1, m, place_all, 0)
    lend.wait()
    add_source(0, False, True)

    def for_twin(u, carry):
        turned(u).wait_recv()
        turned(m + u).start()
        add_source(u, False, True)
        return carry

    def hand_over(c):
        leaving[c] = sums[c].astype(bf16)
        partial(c).start()
        sums[c] = jnp.zeros((2 * TIME, BEAMS), f32)

    lax.fori_loop(1, m - 1, for_twin, 0)
    turned(m - 1).wait_recv()
    turned(n - 1).start()
    add_source(m - 1, False, True, hand_over)
    add_source(m, True, True)

    def for_self(u, carry):
        turned(u).wait_recv()
        add_source(u, True, True)
        return carry

    lax.fori_loop(m + 1, n - 1, for_self, 0)
    turned(n - 1).wait_recv()

    def detect(c):
        partial(c).wait()
        total = sums[c] + landing[c].astype(f32)
        power[c] = total[:TIME] * total[:TIME] + total[TIME:] * total[TIME:]

    add_source(n - 1, True, False, detect)
    flat = power[...].reshape(local * TIME, BEAMS)
    high = flat.astype(bf16)
    low = (flat - high.astype(f32)).astype(bf16)
    chosen = jnp.dot(high, onehot[...], preferred_element_type=f32) + jnp.dot(
        low, onehot[...], preferred_element_type=f32
    )
    chosen = chosen.reshape(local, TIME, TIME * SEARCH) * spread[...][None]
    mine[...] = jnp.sum(chosen, axis=1).astype(bf16)
    here = pl.ds(pl.multiple_of(me * local, local), local)
    gathered[here, :] = mine[...]

    def shared(step):
        return pltpu.make_async_remote_copy(
            src_ref=mine,
            dst_ref=gathered.at[here],
            send_sem=share_send.at[step],
            recv_sem=share_recv.at[step],
            device_id={"crate": peer(step)},
            device_id_type=MESH,
        )

    def share(step, carry):
        shared(step).start()
        return carry

    def drain(u, carry):
        turned(u).wait_send()
        return carry

    def arrive(step, carry):
        shared(step).wait()
        return carry

    lax.fori_loop(1, n, share, 0)
    lax.fori_loop(1, m, drain, 0)
    lax.fori_loop(m + 1, n, drain, 0)
    lax.fori_loop(1, n, arrive, 0)

    everything = gathered[...]
    right = jnp.concatenate([everything[:, : half * SEARCH], everything[:, half * SEARCH :]], axis=0)
    bins = lax.broadcasted_iota(jnp.int32, (2 * trials, half * SEARCH), 1) % half
    out = jnp.zeros((2 * trials, half * SEARCH), f32)
    for k in range(half):
        out = jnp.where(bins == k, jnp.dot(twist[k], right, preferred_element_type=f32), out)
    out = out.T.reshape(SEARCH, half, 2 * trials)
    plane[:, :half, :] = out[:, :, :trials]
    plane[:, half:, :] = out[:, :, trials:]


def crate_device(n, voltages, gains, positions, directions, input_order, delays, search_beams):
    window, dft, spread = constant_tables()
    local = CH // n
    rows = 2 * local
    trials = TRIALS // n
    half = TIME // 2
    f32, bf16 = jnp.float32, jnp.bfloat16
    vmem = pl.BlockSpec(memory_space=pltpu.VMEM)
    power, plane = pl.pallas_call(
        functools.partial(crate_kernel, n),
        out_shape=(
            jax.ShapeDtypeStruct((local, TIME, BEAMS), f32),
            jax.ShapeDtypeStruct((SEARCH, TIME, trials), f32),
        ),
        in_specs=[vmem] * 10,
        out_specs=(vmem, vmem),
        scratch_shapes=[
            pltpu.VMEM((2 * CH, FFTLEN), bf16),
            pltpu.VMEM((TIME // 2, 2 * LANES, FFTLEN), bf16),
            pltpu.VMEM((TIME * 2 * CH, LANES), f32),
            pltpu.VMEM((n, rows, TIME, LANES), bf16),
            pltpu.VMEM((n, rows, TIME, LANES), bf16),
            pltpu.VMEM((48, INPUTS), bf16),
            pltpu.VMEM((n // 2, LANES, LANES), f32),
            pltpu.VMEM((2, local, 2 * LANES, BEAMS), bf16),
            pltpu.VMEM((local, 2 * TIME, BEAMS), f32),
            pltpu.VMEM((half, 2 * trials, 2 * CH), bf16),
            pltpu.VMEM((BEAMS, TIME * SEARCH), bf16),
            pltpu.VMEM((local, TIME * SEARCH), bf16),
            pltpu.VMEM((CH, TIME * SEARCH), bf16),
            pltpu.VMEM((local, 2, INPUTS // 2), f32),
            pltpu.VMEM((local, 2 * TIME, BEAMS), bf16),
            pltpu.VMEM((local, 2 * TIME, BEAMS), bf16),
            pltpu.SemaphoreType.DMA((n,)),
            pltpu.SemaphoreType.DMA((n,)),
            pltpu.SemaphoreType.DMA((2,)),
            pltpu.SemaphoreType.DMA((n,)),
            pltpu.SemaphoreType.DMA((n,)),
            pltpu.SemaphoreType.DMA((2,)),
            pltpu.SemaphoreType.DMA((local,)),
            pltpu.SemaphoreType.DMA((local,)),
        ],
        compiler_params=pltpu.CompilerParams(
            collective_id=0, has_side_effects=True, vmem_limit_bytes=56 * 1024 * 1024
        ),
    )(
        voltages,
        jnp.asarray(window),
        jnp.asarray(dft),
        gains,
        positions,
        directions,
        input_order[None, :],
        delays,
        search_beams[None, :],
        jnp.asarray(spread),
    )
    return jnp.swapaxes(power, 1, 2), plane.transpose(2, 0, 1)


def solution(mesh):
    in_specs = (P(("groups", "crate"), None), P("crate", None, None), P(), P(), P(), P(), P())
    out_specs = (P(("groups", "crate"), None, None), P(("groups", "crate"), None, None))
    n = mesh.shape["crate"]
    fits = n % 4 == 0 and INPUTS // n == LANES and (CH // n) % 16 == 0 and (TRIALS // n) % 16 == 0
    body = functools.partial(crate_device, n) if fits else plain_device
    return jax.shard_map(body, mesh=mesh, in_specs=in_specs, out_specs=out_specs, check_vma=False)
```
